128 devices in a mesh: dp: 8 (over z_lo, y), chan: 16 (over x, z_hi, core).
Axes of the slice: x: 4, y: 4, z: 4 (z_hi: 2, z_lo: 2; z = z_hi * 2 + z_lo), core: 2. Of those that a mesh axis runs over, the one named last changes fastest.
Arguments:
- hidden_in: bfloat16 [8192, 8192], P('dp'), may hold values from -6 to 6
- proj_weight: bfloat16 [8192, 8192], P('dp', 'chan'), may hold values from -0.09375 to 0.09375
- embed: bfloat16 [8192, 8192], P('dp', 'chan')
- embed_grad: bfloat16 [8192, 8192], P('dp', 'chan')
- eigvec: float32 [8192, 512], P('chan'), as said below
- eigval: float32 [8192], P('chan'), as said below
Outputs:
- grad_weight: bfloat16 [8192, 8192], P('dp', 'chan')
- grad_hidden: bfloat16 [8192, 8192], P('dp', 'chan')
The draws below stay inside these ranges and needn't reach their ends.
Inputs may be any that keep to these rules, and one draw needn't show every extreme that they name: `eigvec`: each group's block of 512 consecutive rows is an orthogonal matrix whose columns are that group's saved eigenvectors. `eigval`: each group's 512 saved eigenvalues are positive and any two of them differ by at least one percent of the larger.
All inputs are finite; a program needn't handle non-finite values.
Results may differ from the reference program's by a relative error of at most 0.005.
Values may be sent and summed in bfloat16 or wider, within the bound.
No kernel may reach another device: no remote copies, remote signals or barrier semaphores. Data moves between devices by JAX's collectives and lax.ppermute only.
A program may use at most 192 MiB of HBM per device.

```python
import math
import jax
import jax.numpy as jnp
from jax import lax

C = 512
DIN = 8192
E = 8192
TOKENS = 8192


def cosine_table(width):
    freq = jnp.arange(width, dtype=jnp.int32)[:, None]
    place = jnp.arange(width, dtype=jnp.int32)[None, :]
    phase = (2 * place + 1) * freq % (4 * width)
    table = math.sqrt(2.0 / width) * jnp.cos(math.pi * phase.astype(jnp.float32) / (2.0 * width))
    first = jnp.where(freq == 0, math.sqrt(0.5), 1.0)
    return (table * first).astype(jnp.float32)


def draw_eigvec(key, part):
    key = jax.random.fold_in(key, 11)
    groups = E // C
    perm_keys = jax.random.split(jax.random.fold_in(key, 1), groups)
    perms = jax.vmap(lambda k: jax.random.permutation(k, C))(perm_keys)
    signs = jax.random.randint(jax.random.fold_in(key, 2), (groups, C), 0, 2) * 2 - 1
    transposed = cosine_table(C).T
    picked = jnp.moveaxis(jnp.take(transposed, perms, axis=1), 1, 0)
    blocks = picked * signs[:, :, None].astype(jnp.float32)
    return blocks.reshape(E, C).astype(jnp.float32)


def draw_eigval(key, part):
    key = jax.random.fold_in(key, 12)
    groups = E // C
    perm_keys = jax.random.split(key, groups)
    perms = jax.vmap(lambda k: jax.random.permutation(k, C))(perm_keys).astype(jnp.float32)
    lowest = 0.1
    spread = 200.0
    values = lowest * jnp.exp(math.log(spread) * perms / (C - 1))
    return values.reshape(E).astype(jnp.float32)


def draw_embed(key, part):
    key = jax.random.fold_in(key, 13)
    place = jnp.arange(TOKENS, dtype=jnp.float32) / (TOKENS - 1)
    offsets = 0.2 * jax.random.truncated_normal(jax.random.fold_in(key, 1), -4.0, 4.0, (E,), jnp.float32)
    noise = jax.random.truncated_normal(jax.random.fold_in(key, 2), -5.0, 5.0, (TOKENS, E), jnp.float32)
    ramp = 1.0 + 2.0 * place
    return (ramp[:, None] * offsets[None, :] + noise).astype(jnp.bfloat16)


def draw_embed_grad(key, part):
    key = jax.random.fold_in(key, 14)
    place = jnp.arange(TOKENS, dtype=jnp.float32) / (TOKENS - 1)
    offsets = 0.2 * jax.random.truncated_normal(jax.random.fold_in(key, 1), -4.0, 4.0, (E,), jnp.float32)
    noise = jax.random.truncated_normal(jax.random.fold_in(key, 2), -5.0, 5.0, (TOKENS, E), jnp.float32)
    ramp = 1.0 + 2.0 * place
    return (ramp[:, None] * offsets[None, :] + noise).astype(jnp.bfloat16)


def raised(drawn, stream_key, source, target, blocks, factor):
    owner, partner = [(jnp.arange(drawn.shape[axis_at]) // (drawn.shape[axis_at] // blocks)).reshape([-1 if axis == axis_at else 1 for axis in range(drawn.ndim)]) for axis_at in (source, target)]
    chosen = jax.random.permutation(stream_key, blocks)[partner]
    strong = (owner == chosen) | (owner == (partner + blocks // 2) % blocks)
    return jnp.where(strong, factor * drawn, drawn)


def level_of(stream_key, extent, cuts, low, top_value):
    loudness = 1.0
    for dim, blocks in cuts:
        steps = jax.random.uniform(jax.random.fold_in(jax.random.fold_in(stream_key, 6), dim), (blocks,), jnp.float32, low / len(cuts), top_value / len(cuts))
        loudness = loudness * jnp.repeat(jnp.exp(steps), extent[dim] // blocks).reshape((-1,) + (1,) * (len(extent) - 1 - dim))
    return loudness


def heavy_noise(own_key, dims, scale, bound, cuts, heavy, kind=jnp.bfloat16):
    drawn = scale * jax.random.normal(own_key, dims, jnp.float32)
    if cuts:
        drawn = drawn * level_of(own_key, dims, cuts, -0.22, 0.18)
    return jnp.clip(raised(drawn, jax.random.fold_in(own_key, 3), *heavy), -bound, bound).astype(kind)


def setup_inputs(seed: int = 0) -> dict:
    key_of = jax.random.split(jax.random.key(seed), 7)
    return {
        "hidden_in": heavy_noise(key_of[0], (TOKENS, DIN), 1.0, 6.0, ((0, 8),), (0, 1, 8, 2.0)),
        "proj_weight": heavy_noise(key_of[1], (DIN, E), DIN ** -0.5, 0.09375, ((0, 8), (1, 16)), (1, 0, 16, 2.0)),
        "embed": draw_embed(jax.random.fold_in(key_of[6], 71), 0),
        "embed_grad": draw_embed_grad(jax.random.fold_in(key_of[6], 71), 0),
        "eigvec": draw_eigvec(jax.random.fold_in(key_of[6], 71), 0),
        "eigval": draw_eigval(jax.random.fold_in(key_of[6], 71), 0),
    }


HI = lax.Precision.HIGHEST

def reference(hidden_in, proj_weight, embed, embed_grad, eigvec, eigval):
    rows = embed.shape[0]
    groups = embed.shape[1] // C
    zfull = embed.astype(jnp.float32)
    gfull = embed_grad.astype(jnp.float32)
    mean_z = lax.optimization_barrier(jnp.sum(zfull, axis=0)) / rows
    mean_g = lax.optimization_barrier(jnp.sum(gfull, axis=0)) / rows
    centered = (zfull - mean_z).reshape(rows, groups, C)
    shifted = (gfull - mean_g).reshape(rows, groups, C)
    grouped = gfull.reshape(rows, groups, C)
    dmat = jnp.einsum('bgc,bgd->gcd', centered, grouped, precision=HI)
    sym = 0.5 * (dmat + jnp.swapaxes(dmat, 1, 2))
    vectors = eigvec.reshape(groups, C, C)
    root = jnp.sqrt(eigval).reshape(groups, C)
    whiten = jnp.einsum('gij,gkj->gik', vectors / root[:, None, :], vectors, precision=HI)
    loewner = -1.0 / (root[:, :, None] * root[:, None, :] * (root[:, :, None] + root[:, None, :]))
    half_rot = jnp.einsum('gji,gjk->gik', vectors, sym, precision=HI)
    rotated = jnp.einsum('gik,gkl->gil', half_rot, vectors, precision=HI)
    inner = loewner * rotated
    half_back = jnp.einsum('gij,gjk->gik', vectors, inner, precision=HI)
    dsigma = jnp.einsum('gik,glk->gil', half_back, vectors, precision=HI)
    first = jnp.einsum('bgc,gcd->bgd', shifted, whiten, precision=HI)
    second = jnp.einsum('bgc,gcd->bgd', centered, dsigma, precision=HI)
    grad_z = (first + 2.0 / rows * second).reshape(rows, groups * C).astype(jnp.bfloat16)
    weight_total = lax.dot_general(hidden_in, grad_z, (((0,), (0,)), ((), ())), preferred_element_type=jnp.float32)
    grad_weight = weight_total.astype(jnp.bfloat16)
    input_total = lax.dot_general(grad_z, proj_weight, (((1,), (1,)), ((), ())), preferred_element_type=jnp.float32)
    grad_hidden = input_total.astype(jnp.bfloat16)
    return (grad_weight, grad_hidden)
```

```python
import jax
import jax.numpy as jnp
from jax import lax
from jax.sharding import PartitionSpec as P

HIGH = lax.Precision.HIGH
HI = lax.Precision.HIGHEST
F32 = jnp.float32
BF16 = jnp.bfloat16
AXES = ("dp", "chan")


def place_of(index):
    dp, chan = divmod(index, 16)
    zlo, y = divmod(dp, 4)
    x, rest = divmod(chan, 4)
    zhi, core = divmod(rest, 2)
    return x, y, zhi * 2 + zlo, core


def index_of(x, y, z, core):
    zhi, zlo = divmod(z % 4, 2)
    return (zlo * 4 + y % 4) * 16 + ((x % 4) * 2 + zhi) * 2 + core


def mover(step):
    pairs = [(i, index_of(*step(*place_of(i)))) for i in range(128)]
    return lambda a: lax.ppermute(a, AXES, pairs)


x_up = mover(lambda x, y, z, k: (x + 1, y, z, k))
x_down = mover(lambda x, y, z, k: (x - 1, y, z, k))
y_up = mover(lambda x, y, z, k: (x, y + 1, z, k))
y_down = mover(lambda x, y, z, k: (x, y - 1, z, k))
z_up = mover(lambda x, y, z, k: (x, y, z + 1, k))
z_down = mover(lambda x, y, z, k: (x, y, z - 1, k))
z_flip = [None] + [mover(lambda x, y, z, k, j=j: (x, y, z ^ j, k)) for j in (1, 2, 3)]
swap = mover(lambda x, y, z, k: (x, y, z, 1 - k))


def mm(a, b, ca, cb, precision=None):
    return lax.dot_general(a, b, (((ca,), (cb,)), ((), ())), precision=precision, preferred_element_type=F32)


def bf(a):
    return a.astype(BF16)


def tie(*arrays):
    return lax.optimization_barrier(arrays)


def split(a, parts):
    out = []
    for _ in range(parts):
        head = lax.reduce_precision(a, 8, 7)
        out.append(bf(head))
        a = a - head
    return out


def ring_reduce(blocks, up, down):
    b0, b1, b2, b3 = blocks
    h = b0.shape[0] // 2
    from_down = up(jnp.concatenate([bf(b1[h:]), bf(b2[:h])]))
    from_up = down(jnp.concatenate([bf(b2[h:]), bf(b3[:h])]))
    from_down2 = up(bf(b1[:h] + from_down[h:].astype(F32)))
    from_up2 = down(bf(b3[h:] + from_up[:h].astype(F32)))
    first = b0[:h] + from_up[h:].astype(F32) + from_down2.astype(F32)
    second = b0[h:] + from_down[:h].astype(F32) + from_up2.astype(F32)
    return jnp.concatenate([first, second])


def local(hidden, weight, embed, embed_grad, eigvec, eigval):
    dp, chan = lax.axis_index("dp"), lax.axis_index("chan")
    zlo, y = dp // 4, dp % 4
    x, zhi, core = chan // 4, (chan // 2) % 2, chan % 2
    z = zhi * 2 + zlo
    n_loc = embed.shape[0]
    rows = n_loc * 8
    ch = embed.shape[1]
    feat = hidden.shape[1] // 8
    sub = n_loc // 8

    def hidden_part(r, half, start, size):
        return lax.dynamic_slice(hidden, (start, (half * 4 + (y + r) % 4) * feat), (size, feat))

    mine = jnp.concatenate([hidden_part(r, 1 - zlo, (x * 2 + core) * sub, sub) for r in range(4)], axis=1)
    h0 = jnp.concatenate([z_up(mine[: sub // 2]), z_down(mine[sub // 2 :])])

    half_rows = weight.shape[0] // 2
    w_keep = lax.dynamic_slice(weight, (core * half_rows, 0), (half_rows, ch))
    w_give = lax.dynamic_slice(weight, ((1 - core) * half_rows, 0), (half_rows, ch))
    w1 = jnp.concatenate([w_keep, swap(w_give)], axis=1)

    with jax.named_scope("stats"):
        sum_z = jnp.sum(embed.astype(F32), axis=0)
        sum_g = jnp.sum(embed_grad.astype(F32), axis=0)
        raw = mm(embed, embed_grad, 0, 0)
        part = raw - (sum_z / n_loc)[:, None] * sum_g[None, :]
        sym = 0.5 * (part + part.T)
        rotated = mm(mm(eigvec, sym, 0, 0, HIGH), eigvec, 1, 0, HIGH)
        q = ch // 4
        sums = jnp.stack([sum_z, sum_g])
        sums3 = jnp.concatenate(split(sums, 3) + [jnp.zeros((10, ch), BF16)])
        message = jnp.concatenate(
            [bf(rotated).reshape(4, q, ch), jnp.broadcast_to(sums3[None], (4, 16, ch))], axis=1
        )
        message, h0, w1 = tie(message, h0, w1)
        groups = [[0, 1, 2, 3], [4, 5, 6, 7]]
        fs = half_rows // 4
        wz = [lax.dynamic_slice(w1, ((z ^ j) * fs, 0), (fs, 2 * ch)) for j in range(4)]
        wz = [wz[0]] + [z_flip[j](wz[j]) for j in (1, 2, 3)]
        w_own = jnp.stack([jnp.concatenate([wz[0], wz[2]], axis=1), jnp.concatenate([wz[1], wz[3]], axis=1)])
        h_left, h_right = x_up(h0), x_down(h0)
        got = lax.all_to_all(message, "dp", 0, 0, axis_index_groups=groups)
        quarter = jnp.sum(got[:, :q].astype(F32), axis=0)
        small = got[:, q:].reshape(64, ch)
        sent, w_own = tie(jnp.concatenate([bf(quarter), small]), w_own)
        w_left, w_right = y_up(w_own), y_down(w_own)
        other = z_flip[1](sent)
        quarter = quarter + other[:q].astype(F32)
        small = jnp.concatenate([small, other[q:]]).reshape(8, 8, 2, ch).astype(F32)
        sums_all = small[:, 0] + small[:, 1] + small[:, 2]
        mean_z = jnp.sum(sums_all[:, 0], axis=0) / rows
        mean_g = jnp.sum(sums_all[:, 1], axis=0) / rows
        dev_z = sums_all[:, 0] - n_loc * mean_z
        dev_g = sums_all[:, 1] / n_loc
        turned = mm(jnp.concatenate([dev_z, dev_g]), eigvec, 1, 0, HI)
        turned_q = lax.dynamic_slice(turned, (0, y * q), (16, q))
        swapped = jnp.concatenate([turned[8:], turned[:8]])
        quarter = quarter + 0.5 * mm(turned_q, swapped, 0, 0, HI)
        root = jnp.sqrt(eigval)
        root_q = lax.dynamic_slice(root, (y * q,), (q,))
        loewner = -1.0 / (root_q[:, None] * root[None, :] * (root_q[:, None] + root[None, :]))
        inner_q, h_left, h_right = tie(bf(loewner * quarter), h_left, h_right)
        h_two_a = x_up(h_left[: sub // 2])
        h_two_b = x_down(h_right[sub // 2 :])
        inner = lax.all_to_all(
            jnp.broadcast_to(inner_q[None], (4, q, ch)), "dp", 0, 0, axis_index_groups=groups
        ).reshape(ch, ch)
        dsigma = mm(mm(eigvec, inner.astype(F32), 1, 0, HIGH), eigvec, 1, 1, HIGH) * (2.0 / rows)
        whiten = mm(eigvec / root[None, :], eigvec, 1, 1, HI)
        dsigma, w_left, w_right, h_two_a, h_two_b = tie(dsigma, w_left, w_right, h_two_a, h_two_b)
    w_two = jnp.concatenate([y_up(w_left[:1]), y_down(w_right[1:])])
    h_x = jnp.concatenate([h0, h_right, h_two_a, h_two_b, h_left])
    h_k = swap(h_x)
    with jax.named_scope("grad_z"):
        wh, wl = split(whiten, 2)
        first = mm(embed_grad, wh, 1, 0) + mm(embed_grad, wl, 1, 0)
        dh, dl = split(dsigma, 2)
        wsum = wh.astype(F32) + wl.astype(F32)
        dsum = dh.astype(F32) + dl.astype(F32)
        bias = mm(mean_g[None], wsum, 1, 0, HI) + mm(mean_z[None], dsum, 1, 0, HI)
        grad_z = bf(first + mm(embed, dh, 1, 0) + mm(embed, dl, 1, 0) - bias)

    w_ring = jnp.stack([w_own, w_right, w_two, w_left])
    w_rows = []
    for r in range(4):
        xr = (x + r) % 4
        for f in range(2):
            y_s = 2 * (xr % 2) + (zhi ^ f)
            w_rows.append(
                lax.dynamic_slice(w_ring, ((y_s - y) % 4, (xr // 2) ^ zlo, 0, 0), (1, 1, fs, 4 * ch)).reshape(fs, 4 * ch)
            )
    w_all = jnp.concatenate(w_rows)


    hc, ht = ch // 2, n_loc // 2
    cols = [grad_z[:, :hc], grad_z[:, hc:]]
    r_own = [z_flip[1](c) for c in cols]
    r_oth = [z_flip[3](c) for c in cols]
    own2 = swap(grad_z)
    r_far = [jnp.concatenate([z_flip[1](r_oth[c][:ht]), z_flip[3](r_own[c][ht:])]) for c in range(2)]

    pieces = []
    for c in range(2):
        q_rows = []
        for k in (core, 1 - core):
            for r in range(4):
                q_rows.append(lax.dynamic_slice(r_own[c], ((((x + r) % 4) * 2 + k) * sub, 0), (sub, hc)))
        q_own = jnp.concatenate(q_rows)
        blocks = []
        for r in range(4):
            col = slice(r * feat, (r + 1) * feat)
            block = mm(cols[c], hidden_part(r, zlo, 0, n_loc), 0, 0)
            block = block + mm(q_own[: n_loc // 2], h_x[:, col], 0, 0)
            block = block + mm(q_own[n_loc // 2 :], h_k[:, col], 0, 0)
            blocks.append(block)
        pieces.append(ring_reduce(blocks, y_up, y_down))
    grad_weight = bf(jnp.concatenate(pieces).T)

    near = jnp.concatenate(r_own + r_oth, axis=1)
    near2 = swap(near)
    a_par = jnp.concatenate([near[:, :ch], near2[:, :ch], near[:, ch:], near2[:, ch:]], axis=1)
    far = jnp.concatenate(r_far, axis=1)
    a_own = jnp.concatenate([grad_z, own2, far, swap(far)], axis=1)

    def reduced(a):
        out = mm(a, w_all, 1, 1)
        return bf(ring_reduce([out[:, 2 * fs * r : 2 * fs * (r + 1)] for r in range(4)], x_up, x_down))

    s_par = reduced(a_par)
    p1 = z_flip[1](s_par[:, :fs])
    p3 = z_flip[3](s_par[:, fs:])
    s_own = reduced(a_own)
    p0 = s_own[:, :fs]
    p2 = z_flip[2](s_own[:, fs:])
    odd = zlo == 1
    u0, u1 = jnp.where(odd, p1, p0), jnp.where(odd, p0, p1)
    u2, u3 = jnp.where(odd, p3, p2), jnp.where(odd, p2, p3)
    low = jnp.concatenate([u0, u1], axis=1)
    high = jnp.concatenate([u2, u3], axis=1)
    up = zhi == 1
    grad_hidden = jnp.concatenate([jnp.where(up, high, low), jnp.where(up, low, high)], axis=1)
    return grad_weight, grad_hidden


def solution(mesh):
    in_specs = (
        P("dp", None),
        P("dp", "chan"),
        P("dp", "chan"),
        P("dp", "chan"),
        P("chan", None),
        P("chan"),
    )
    out_specs = (P("dp", "chan"), P("dp", "chan"))
    return jax.shard_map(local, mesh=mesh, in_specs=in_specs, out_specs=out_specs, check_vma=False)
```

```python
import functools

import jax
import jax.numpy as jnp
from jax import lax
from jax.experimental import pallas as pl
from jax.experimental.pallas import tpu as pltpu
from jax.sharding import PartitionSpec as P

F32 = jnp.float32
BF16 = jnp.bfloat16
AXES = ("dp", "chan")


def place_of(index):
    dp, chan = divmod(index, 16)
    zlo, y = divmod(dp, 4)
    x, rest = divmod(chan, 4)
    zhi, core = divmod(rest, 2)
    return x, y, zhi * 2 + zlo, core


def index_of(x, y, z, core):
    zhi, zlo = divmod(z % 4, 2)
    return (zlo * 4 + y % 4) * 16 + ((x % 4) * 2 + zhi) * 2 + core


def mover(step):
    pairs = [(i, index_of(*step(*place_of(i)))) for i in range(128)]
    return lambda a: lax.ppermute(a, AXES, pairs)


x_up = mover(lambda x, y, z, k: (x + 1, y, z, k))
x_down = mover(lambda x, y, z, k: (x - 1, y, z, k))
y_up = mover(lambda x, y, z, k: (x, y + 1, z, k))
y_down = mover(lambda x, y, z, k: (x, y - 1, z, k))
z_up = mover(lambda x, y, z, k: (x, y, z + 1, k))
z_down = mover(lambda x, y, z, k: (x, y, z - 1, k))
z_flip = [None] + [mover(lambda x, y, z, k, j=j: (x, y, z ^ j, k)) for j in (1, 2, 3)]
swap = mover(lambda x, y, z, k: (x, y, z, 1 - k))


def bf(a):
    return a.astype(BF16)


def tie(*arrays):
    return lax.optimization_barrier(arrays)


def halves(a):
    head = bf(a)
    return head, bf(a - head.astype(F32))


def dot(a, b, ca, cb):
    return lax.dot_general(a, b, (((ca,), (cb,)), ((), ())), preferred_element_type=F32)


def dot3(a, b, ca, cb):
    (ah, al), (bh, bl) = halves(a), halves(b)
    return dot(ah, bh, ca, cb) + (dot(ah, bl, ca, cb) + dot(al, bh, ca, cb))


def hbm(*arrays):
    return [pltpu.with_memory_space_constraint(a, pltpu.HBM) for a in arrays]


def params(mib):
    return pltpu.CompilerParams(vmem_limit_bytes=mib * 2**20)


def cost(flops, nbytes):
    return pl.CostEstimate(flops=int(flops), bytes_accessed=int(nbytes), transcendentals=0)


def moments_kernel(z_ref, g_ref, u_ref, out_ref):
    n_loc, ch = z_ref.shape
    q = ch // 4
    z, g = z_ref[...], g_ref[...]
    sum_z = jnp.sum(z.astype(F32), axis=0, keepdims=True)
    sum_g = jnp.sum(g.astype(F32), axis=0, keepdims=True)
    zero = jnp.zeros((7, ch), F32)
    outer = dot3(jnp.concatenate([sum_z * (1.0 / n_loc), zero]), jnp.concatenate([sum_g, zero]), 0, 0)
    part = dot(z, g, 0, 0) - outer
    sym = 0.5 * (part + part.T)
    u = u_ref[...]
    rotated = dot3(dot3(u, sym, 0, 0), u, 1, 0)
    sums = jnp.concatenate([sum_z, sum_g])
    parts = []
    for _ in range(3):
        head = bf(sums).astype(F32)
        parts.append(head)
        sums = sums - head
    small = bf(jnp.concatenate(parts + [jnp.zeros((10, ch), F32)]))
    for r in range(4):
        out_ref[r, :q, :] = bf(rotated[r * q : (r + 1) * q])
        out_ref[r, q:, :] = small


def moments(embed, embed_grad, eigvec):
    n_loc, ch = embed.shape
    return pl.pallas_call(
        moments_kernel,
        out_shape=pltpu.HBM((4, ch // 4 + 16, ch), BF16),
        compiler_params=params(20),
        cost_estimate=cost(2 * n_loc * ch * ch + 12 * ch**3, 4 * n_loc * ch + 6 * ch * ch),
    )(*hbm(embed, embed_grad, eigvec))


def quarter_kernel(got_ref, quarter_ref, sent_ref):
    q = quarter_ref.shape[0]
    total = sum(got_ref[r, :q, :].astype(F32) for r in range(4))
    quarter_ref[...] = total
    sent_ref[:q, :] = bf(total)
    for r in range(4):
        sent_ref[q + 16 * r : q + 16 * (r + 1), :] = got_ref[r, q:, :]


def inner_kernel(y_ref, quarter_ref, sent_ref, other_ref, u_ref, uq_ref, root_ref, rootq_ref, inner_ref, mean_ref, *, n_loc):
    q, ch = quarter_ref.shape
    first, second = [], []
    for ref in (sent_ref, other_ref):
        small = ref[q:, :].astype(F32)
        for r in range(4):
            block = small[16 * r : 16 * r + 16]
            both = block[0:2] + block[2:4] + block[4:6]
            first.append(both[0:1])
            second.append(both[1:2])
    sum_z, sum_g = jnp.concatenate(first), jnp.concatenate(second)
    mean_z = jnp.sum(sum_z, axis=0, keepdims=True) * (1.0 / (8 * n_loc))
    mean_g = jnp.sum(sum_g, axis=0, keepdims=True) * (1.0 / (8 * n_loc))
    dev_z = sum_z - n_loc * mean_z
    dev_g = sum_g * (1.0 / n_loc)
    turned = dot3(jnp.concatenate([dev_g, dev_z]), u_ref[...], 1, 0)
    turned_q = dot3(jnp.concatenate([dev_z, dev_g]), uq_ref[...], 1, 0)
    total = quarter_ref[...] + other_ref[:q, :].astype(F32) + 0.5 * dot3(turned_q, turned, 0, 0)
    root, rootq = root_ref[...], rootq_ref[...]
    inner = bf(total * (-1.0 / (rootq * root * (rootq + root))))
    for r in range(4):
        inner_ref[r] = inner
    mean_ref[...] = jnp.concatenate([mean_z, mean_g, jnp.zeros((6, ch), F32)])


def quarter_terms(got):
    ch = got.shape[2]
    q = ch // 4
    return pl.pallas_call(
        quarter_kernel,
        out_shape=(pltpu.HBM((q, ch), F32), pltpu.HBM((q + 64, ch), BF16)),
        compiler_params=params(8),
    )(*hbm(got))


def inner_terms(quarter, sent, other, eigvec, root, y, n_loc):
    q, ch = quarter.shape
    full = lambda *shape: pl.BlockSpec(shape, lambda i, y: (0,) * len(shape))
    return pl.pallas_call(
        functools.partial(inner_kernel, n_loc=n_loc),
        out_shape=(pltpu.HBM((4, q, ch), BF16), pltpu.HBM((8, ch), F32)),
        grid_spec=pltpu.PrefetchScalarGridSpec(
            num_scalar_prefetch=1,
            grid=(1,),
            in_specs=[
                full(q, ch),
                full(q + 64, ch),
                full(q + 64, ch),
                full(ch, ch),
                pl.BlockSpec((ch, q), lambda i, y: (0, y[0])),
                full(1, ch),
                pl.BlockSpec((q, 1), lambda i, y: (y[0], 0)),
            ],
            out_specs=(full(4, q, ch), full(8, ch)),
        ),
        compiler_params=params(16),
    )(y.reshape(1), *hbm(quarter, sent, other, eigvec, eigvec), root[None, :], root[:, None])


def first_kernel(u_ref, root_ref, g_ref, wsum_ref, first_ref):
    u = u_ref[...]
    whiten = dot3(u / root_ref[...], u, 1, 1)
    wh, wl = halves(whiten)
    wsum_ref[...] = wh.astype(F32) + wl.astype(F32)
    g = g_ref[...]
    first_ref[...] = dot(g, wh, 1, 0) + dot(g, wl, 1, 0)


def first_terms(eigvec, root, embed_grad):
    n_loc, ch = embed_grad.shape
    return pl.pallas_call(
        first_kernel,
        out_shape=(pltpu.HBM((ch, ch), F32), pltpu.HBM((n_loc, ch), F32)),
        compiler_params=params(14),
        cost_estimate=cost(6 * ch**3 + 4 * n_loc * ch * ch, 6 * n_loc * ch + 8 * ch * ch),
    )(*hbm(eigvec), root[None, :], *hbm(embed_grad))


def grad_z_kernel(u_ref, inner_ref, z_ref, first_ref, wsum_ref, mean_ref, out_ref, turned_ref, *, scale):
    u, inner = u_ref[...], inner_ref[...]
    uh, ul = halves(u)
    back = dot(uh, inner, 1, 0) + dot(ul, inner, 1, 0)
    dsigma = dot3(back, u, 1, 1) * scale
    dh, dl = halves(dsigma)
    mean = mean_ref[...]
    bias = dot3(mean, wsum_ref[...], 1, 0)[1:2] + dot3(mean, dh.astype(F32) + dl.astype(F32), 1, 0)[0:1]
    z = z_ref[...]
    out = first_ref[...] + dot(z, dh, 1, 0) + dot(z, dl, 1, 0) - bias
    out_ref[...] = bf(out)
    turned_ref[...] = bf(out.T)


def grad_z_of(eigvec, inner, embed, first, wsum, means, rows):
    n_loc, ch = embed.shape
    return pl.pallas_call(
        functools.partial(grad_z_kernel, scale=2.0 / rows),
        out_shape=(pltpu.HBM((n_loc, ch), BF16), pltpu.HBM((ch, n_loc), BF16)),
        compiler_params=params(20),
        cost_estimate=cost(10 * ch**3 + 4 * n_loc * ch * ch, 8 * n_loc * ch + 10 * ch * ch),
    )(*hbm(eigvec, inner, embed, first, wsum), means)


def ring_shapes(rows, cols):
    half = rows // 2
    return (
        pltpu.HBM((rows, cols), BF16),
        pltpu.HBM((rows, cols), BF16),
        pltpu.HBM((rows, cols), F32),
        pltpu.HBM((half, cols), F32),
        pltpu.HBM((half, cols), F32),
    )


def ring_store(r, start, acc, up_ref, down_ref, b0_ref, b1_ref, b3_ref, cols=slice(None)):
    size, half = acc.shape[0], b1_ref.shape[0]
    lower = start < half
    at = pl.ds(start % half, size)
    later = pl.ds(half + start % half, size)

    @pl.when(r == 0)
    def _():
        b0_ref[pl.ds(start, size), cols] = acc

    @pl.when(r == 1)
    def _():
        if lower:
            b1_ref[at, cols] = acc
        else:
            up_ref[at, cols] = bf(acc)

    @pl.when(r == 2)
    def _():
        if lower:
            up_ref[later, cols] = bf(acc)
        else:
            down_ref[at, cols] = bf(acc)

    @pl.when(r == 3)
    def _():
        if lower:
            down_ref[later, cols] = bf(acc)
        else:
            b3_ref[at, cols] = acc


def order_kernel(idx_ref, own_ref, right_ref, two_a_ref, two_b_ref, left_ref, out_ref, sems):
    fs = own_ref.shape[2]
    for g in range(8):
        place, side = idx_ref[g] // 2, idx_ref[g] % 2
        to, sem = out_ref.at[:, g * fs : (g + 1) * fs], sems.at[g]
        for n, ref in ((0, own_ref), (1, right_ref), (3, left_ref)):

            @pl.when(place == n)
            def _():
                pltpu.make_async_copy(ref.at[side], to, sem).start()

        for n, ref in ((0, two_a_ref), (1, two_b_ref)):

            @pl.when((place == 2) & (side == n))
            def _():
                pltpu.make_async_copy(ref.at[0], to, sem).start()

    for g in range(8):
        to, sem = out_ref.at[:, g * fs : (g + 1) * fs], sems.at[g]
        pltpu.make_async_copy(own_ref.at[0], to, sem).wait()


def in_order(sources, order):
    _, depth, fs = sources[0].shape
    return pl.pallas_call(
        order_kernel,
        out_shape=jax.ShapeDtypeStruct((depth, 8 * fs), BF16),
        in_specs=[pl.BlockSpec(memory_space=pltpu.SMEM)] + [pl.BlockSpec(memory_space=pl.ANY)] * 5,
        out_specs=pl.BlockSpec(memory_space=pl.ANY),
        scratch_shapes=[pltpu.SemaphoreType.DMA((8,))],
        compiler_params=params(4),
    )(order, *sources)


def stack_kernel(*refs):
    *sources, out_ref = refs
    at = 0
    for ref in sources:
        out_ref[at : at + ref.shape[0], :] = ref[...]
        at += ref.shape[0]


def stacked(sources):
    rows = sum(a.shape[0] for a in sources)
    return pl.pallas_call(
        stack_kernel,
        out_shape=pltpu.HBM((rows, sources[0].shape[1]), BF16),
        compiler_params=params(12),
    )(*sources)


def halves_kernel(core_ref, keep_in, give_in, keep_ref, give_ref):
    keep_ref[...] = bf(keep_in[...].astype(F32).T)
    give_ref[...] = bf(give_in[...].astype(F32).T)


def turned_halves(weight, core):
    rows, ch = weight.shape
    half = rows // 2
    shape = jax.ShapeDtypeStruct((ch, half), BF16)
    return pl.pallas_call(
        halves_kernel,
        out_shape=(shape, shape),
        grid_spec=pltpu.PrefetchScalarGridSpec(
            num_scalar_prefetch=1,
            grid=(1,),
            in_specs=[
                pl.BlockSpec((half, ch), lambda i, c: (c[0], 0)),
                pl.BlockSpec((half, ch), lambda i, c: (1 - c[0], 0)),
            ],
            out_specs=tuple(pl.BlockSpec((ch, half), lambda i, c: (0, 0)) for _ in range(2)),
        ),
        compiler_params=params(12),
    )(core.reshape(1), weight, weight)


def hidden_kernel(*refs):
    *lhs, w_ref, out_ref = refs
    _, rows, wide = out_ref.shape
    tile = rows // 2
    for start in range(0, rows, tile):
        acc, k0 = None, 0
        for ref in lhs:
            depth = ref.shape[1]
            term = dot(ref[start : start + tile, :], w_ref[k0 : k0 + depth, :], 1, 0)
            acc = term if acc is None else acc + term
            k0 += depth
        for r in range(4):
            out_ref[r, start : start + tile, :] = bf(acc[:, r * wide : (r + 1) * wide])


def hidden_terms(pieces, w_all):
    rows = pieces[0].shape[0]
    depth, wide = w_all.shape
    return pl.pallas_call(
        hidden_kernel,
        out_shape=pltpu.HBM((4, rows, wide // 4), BF16),
        compiler_params=params(20),
        cost_estimate=cost(2 * rows * wide * depth, 2 * (rows + wide) * depth + 2 * rows * wide),
    )(*pieces, w_all)


def here_kernel(idx_ref, p_ref, own_ref, out_ref):
    out_ref[...] = dot(p_ref[...], own_ref[...], 1, 0)


def weight_here(turned, hidden, order):
    ch, n_loc = turned.shape
    feat = hidden.shape[1] // 8
    return pl.pallas_call(
        here_kernel,
        out_shape=pltpu.HBM((ch, 4 * feat), F32),
        grid_spec=pltpu.PrefetchScalarGridSpec(
            num_scalar_prefetch=1,
            grid=(4,),
            in_specs=[
                pl.BlockSpec((ch, n_loc), lambda r, idx: (0, 0)),
                pl.BlockSpec((n_loc, feat), lambda r, idx: (0, idx[r])),
            ],
            out_specs=pl.BlockSpec((ch, feat), lambda r, idx: (0, r)),
        ),
        compiler_params=params(14),
        cost_estimate=cost(8 * ch * n_loc * feat, 8 * feat * (n_loc + 2 * ch)),
    )(order, *hbm(turned, hidden))


def weight_kernel(idx_ref, q_ref, own_ref, hx_ref, hk_ref, up_ref, down_ref, b0_ref, b1_ref, b3_ref, turned_ref):
    r = pl.program_id(0)
    core, x = idx_ref[4], idx_ref[5]
    half = hx_ref.shape[0]
    h = b1_ref.shape[0]
    sub = half // 4

    @pl.when(r == 0)
    def _():
        for n in range(8):
            k = core if n < 4 else 1 - core
            row = pl.multiple_of((k * 4 + (x + n) % 4) * sub, sub)
            turned_ref[:, n * sub : (n + 1) * sub] = bf(q_ref[pl.ds(row, sub), :].astype(F32).T)

    acc = own_ref[...] + dot(turned_ref[:, :half], hx_ref[...], 1, 0) + dot(turned_ref[:, half:], hk_ref[...], 1, 0)
    for start in (0, h):
        ring_store(r, start, acc[start : start + h], up_ref, down_ref, b0_ref, b1_ref, b3_ref)


def weight_terms(q_own, w_here, h_x, h_k, order):
    n_loc, ch = q_own.shape
    feat = h_x.shape[1] // 4
    shapes = ring_shapes(ch, feat)
    whole = lambda a: pl.BlockSpec(a.shape, lambda r, idx: (0, 0))
    return pl.pallas_call(
        weight_kernel,
        out_shape=shapes,
        grid_spec=pltpu.PrefetchScalarGridSpec(
            num_scalar_prefetch=1,
            grid=(4,),
            in_specs=[
                whole(q_own),
                pl.BlockSpec((ch, feat), lambda r, idx: (0, r)),
                pl.BlockSpec((n_loc // 2, feat), lambda r, idx: (0, r)),
                pl.BlockSpec((n_loc // 2, feat), lambda r, idx: (0, r)),
            ],
            out_specs=tuple(whole(a) for a in shapes),
            scratch_shapes=[pltpu.VMEM((ch, n_loc), BF16)],
        ),
        compiler_params=params(30),
        cost_estimate=cost(8 * n_loc * feat * ch, 8 * n_loc * feat + 28 * ch * feat),
    )(order, q_own, *hbm(w_here, h_x, h_k))


def ring_finish(terms, first, up, down):
    _, _, b0, b1, b3 = terms
    from_down, from_up = first
    h = b1.shape[0]
    from_down2 = up(bf(b1 + from_down[h:].astype(F32)))
    from_up2 = down(bf(b3 + from_up[:h].astype(F32)))
    lower = b0[:h] + from_up[h:].astype(F32) + from_down2.astype(F32)
    upper = b0[h:] + from_down[:h].astype(F32) + from_up2.astype(F32)
    return jnp.concatenate([lower, upper])


def local(hidden, weight, embed, embed_grad, eigvec, eigval):
    dp, chan = lax.axis_index("dp"), lax.axis_index("chan")
    zlo, y = dp // 4, dp % 4
    x, zhi, core = chan // 4, (chan // 2) % 2, chan % 2
    z = zhi * 2 + zlo
    n_loc = embed.shape[0]
    rows = n_loc * 8
    ch = embed.shape[1]
    feat = hidden.shape[1] // 8
    sub = n_loc // 8

    groups = [[0, 1, 2, 3], [4, 5, 6, 7]]
    x_groups = [[(i * 2 + a) * 2 + b for i in range(4)] for a in range(2) for b in range(2)]
    message, hidden, weight = tie(moments(embed, embed_grad, eigvec), hidden, weight)
    got = lax.all_to_all(message, "dp", 0, 0, axis_index_groups=groups)

    def hidden_part(r, half, start, size):
        return lax.dynamic_slice(hidden, (start, (half * 4 + (y + r) % 4) * feat), (size, feat))

    mine = jnp.concatenate([hidden_part(r, 1 - zlo, (core * 4 + x) * sub, sub) for r in range(4)], axis=1)
    h0 = stacked([z_up(mine[: sub // 2]), z_down(mine[sub // 2 :])])

    half_rows = weight.shape[0] // 2
    fs = half_rows // 4
    w_keep, w_give = turned_halves(weight, core)
    w1 = jnp.concatenate([w_keep, swap(w_give)])
    got, h0, w1 = tie(got, h0, w1)
    h_left, h_right = x_up(h0), x_down(h0)
    quarter, sent = quarter_terms(got)
    other = z_flip[1](sent)
    root = jnp.sqrt(eigval)
    root, _ = tie(root, quarter)
    wsum, first = first_terms(eigvec, root, embed_grad)
    other, first, wsum = tie(other, first, wsum)
    inner4, means = inner_terms(quarter, sent, other, eigvec, root, y, n_loc)
    inner4, w1 = tie(inner4, w1)
    inner = lax.all_to_all(inner4, "dp", 0, 0, axis_index_groups=groups).reshape(ch, ch)
    wz = [lax.dynamic_slice(w1, (0, (z ^ j) * fs), (2 * ch, fs)) for j in range(4)]
    wz = [wz[0]] + [z_flip[j](wz[j]) for j in (1, 2, 3)]
    inner, h_left, h_right, *wz = tie(inner, h_left, h_right, *wz)
    w_own = jnp.stack([jnp.concatenate([wz[0], wz[2]]), jnp.concatenate([wz[1], wz[3]])])
    w_left, w_right = y_up(w_own), y_down(w_own)
    h_two = x_up(h_left[: sub // 2]), x_down(h_right[sub // 2 :])
    grad_z, turned = grad_z_of(eigvec, inner, embed, first, wsum, means, rows)

    w_order = []
    for r in range(4):
        for f in range(2):
            y_s = 2 * (r % 2) + (zhi ^ f)
            w_order.append(((y_s - y) % 4) * 2 + ((r // 2) ^ zlo))
    w_order = jnp.stack(w_order).astype(jnp.int32)
    h_order = jnp.stack([zlo * 4 + (y + r) % 4 for r in range(4)] + [core, x]).astype(jnp.int32)

    ht = n_loc // 2
    r_own = z_flip[1](grad_z)
    r_oth = z_flip[3](grad_z)
    own2 = swap(grad_z)
    w_here = weight_here(turned, hidden, h_order)
    w_two = y_up(w_left[:1]), y_down(w_right[1:])
    r_own, r_oth, w_here, *two = tie(r_own, r_oth, w_here, *w_two, *h_two)
    w_two, h_two = two[:2], two[2:]
    h_x = stacked([h0, h_right, *h_two, h_left])
    h_k = swap(h_x)
    w_all = in_order([w_own, w_right, *w_two, w_left], w_order)

    far = z_flip[1](r_oth[:ht]), z_flip[3](r_own[ht:])
    par = hidden_terms([r_own, swap(r_own), r_oth, swap(r_oth)], w_all)
    par, *far = tie(par, *far)
    par_got = lax.all_to_all(par, "chan", 0, 0, axis_index_groups=x_groups)

    r_own, _ = tie(r_own, par)
    w_terms = weight_terms(r_own, w_here, h_x, h_k, h_order)
    w_first = y_up(w_terms[0]), y_down(w_terms[1])

    far = jnp.concatenate(far)
    far2 = swap(far)
    grad_z, _ = tie(grad_z, w_terms[0])
    own = hidden_terms([grad_z, own2, far, far2], w_all)
    own, par_got = tie(own, par_got)
    own_got = lax.all_to_all(own, "chan", 0, 0, axis_index_groups=x_groups)
    s_par = bf(jnp.sum(par_got.astype(F32), axis=0))
    p1 = z_flip[1](s_par[:, :fs])
    p3 = z_flip[3](s_par[:, fs:])
    w_sum = ring_finish(w_terms, w_first, y_up, y_down)
    s_own = bf(jnp.sum(own_got.astype(F32), axis=0))
    p0 = s_own[:, :fs]
    p2 = z_flip[2](s_own[:, fs:])
    grad_weight = bf(w_sum.T)
    odd = zlo == 1
    u0, u1 = jnp.where(odd, p1, p0), jnp.where(odd, p0, p1)
    u2, u3 = jnp.where(odd, p3, p2), jnp.where(odd, p2, p3)
    low = jnp.concatenate([u0, u1], axis=1)
    high = jnp.concatenate([u2, u3], axis=1)
    up = zhi == 1
    grad_hidden = jnp.concatenate([jnp.where(up, high, low), jnp.where(up, low, high)], axis=1)
    return grad_weight, grad_hidden


def solution(mesh):
    in_specs = (
        P("dp", None),
        P("dp", "chan"),
        P("dp", "chan"),
        P("dp", "chan"),
        P("chan", None),
        P("chan"),
    )
    out_specs = (P("dp", "chan"), P("dp", "chan"))
    return jax.shard_map(local, mesh=mesh, in_specs=in_specs, out_specs=out_specs, check_vma=False)
```

```python
import functools

import jax
import jax.numpy as jnp
from jax import lax
from jax.experimental import pallas as pl
from jax.experimental.pallas import tpu as pltpu
from jax.sharding import PartitionSpec as P

F32 = jnp.float32
BF16 = jnp.bfloat16
AXES = ("dp", "chan")


def place_of(index):
    dp, chan = divmod(index, 16)
    zlo, y = divmod(dp, 4)
    x, rest = divmod(chan, 4)
    zhi, core = divmod(rest, 2)
    return x, y, zhi * 2 + zlo, core


def index_of(x, y, z, core):
    zhi, zlo = divmod(z % 4, 2)
    return (zlo * 4 + y % 4) * 16 + ((x % 4) * 2 + zhi) * 2 + core


def mover(step):
    pairs = [(i, index_of(*step(*place_of(i)))) for i in range(128)]
    return lambda a: lax.ppermute(a, AXES, pairs)


x_up = mover(lambda x, y, z, k: (x + 1, y, z, k))
x_down = mover(lambda x, y, z, k: (x - 1, y, z, k))
y_up = mover(lambda x, y, z, k: (x, y + 1, z, k))
y_down = mover(lambda x, y, z, k: (x, y - 1, z, k))
z_up = mover(lambda x, y, z, k: (x, y, z + 1, k))
z_down = mover(lambda x, y, z, k: (x, y, z - 1, k))
z_flip = [None] + [mover(lambda x, y, z, k, j=j: (x, y, z ^ j, k)) for j in (1, 2, 3)]
swap = mover(lambda x, y, z, k: (x, y, z, 1 - k))


def bf(a):
    return a.astype(BF16)


def tie(*arrays):
    return lax.optimization_barrier(arrays)


def halves(a):
    head = bf(a)
    return head, bf(a - head.astype(F32))


def dot(a, b, ca, cb):
    return lax.dot_general(a, b, (((ca,), (cb,)), ((), ())), preferred_element_type=F32)


def dot3(a, b, ca, cb):
    (ah, al), (bh, bl) = halves(a), halves(b)
    return dot(ah, bh, ca, cb) + (dot(ah, bl, ca, cb) + dot(al, bh, ca, cb))


def hbm(*arrays):
    return [pltpu.with_memory_space_constraint(a, pltpu.HBM) for a in arrays]


def params(mib):
    return pltpu.CompilerParams(vmem_limit_bytes=mib * 2**20)


def cost(flops, nbytes):
    return pl.CostEstimate(flops=int(flops), bytes_accessed=int(nbytes), transcendentals=0)


def moments_kernel(z_ref, g_ref, u_ref, out_ref):
    n_loc, ch = z_ref.shape
    q = ch // 4
    z, g = z_ref[...], g_ref[...]
    sum_z = jnp.sum(z.astype(F32), axis=0, keepdims=True)
    sum_g = jnp.sum(g.astype(F32), axis=0, keepdims=True)
    zero = jnp.zeros((7, ch), F32)
    outer = dot3(jnp.concatenate([sum_z * (1.0 / n_loc), zero]), jnp.concatenate([sum_g, zero]), 0, 0)
    part = dot(z, g, 0, 0) - outer
    sym = 0.5 * (part + part.T)
    u = u_ref[...]
    rotated = dot3(dot3(u, sym, 0, 0), u, 1, 0)
    sums = jnp.concatenate([sum_z, sum_g])
    parts = []
    for _ in range(3):
        head = bf(sums).astype(F32)
        parts.append(head)
        sums = sums - head
    small = bf(jnp.concatenate(parts + [jnp.zeros((10, ch), F32)]))
    for r in range(4):
        out_ref[r, :q, :] = bf(rotated[r * q : (r + 1) * q])
        out_ref[r, q:, :] = small


def moments(embed, embed_grad, eigvec):
    n_loc, ch = embed.shape
    return pl.pallas_call(
        moments_kernel,
        out_shape=pltpu.HBM((4, ch // 4 + 16, ch), BF16),
        compiler_params=params(20),
        cost_estimate=cost(2 * n_loc * ch * ch + 12 * ch**3, 4 * n_loc * ch + 6 * ch * ch),
    )(*hbm(embed, embed_grad, eigvec))


def quarter_kernel(got_ref, quarter_ref, sent_ref):
    q = quarter_ref.shape[0]
    total = sum(got_ref[r, :q, :].astype(F32) for r in range(4))
    quarter_ref[...] = total
    sent_ref[:q, :] = bf(total)
    for r in range(4):
        sent_ref[q + 16 * r : q + 16 * (r + 1), :] = got_ref[r, q:, :]


def inner_kernel(y_ref, quarter_ref, sent_ref, other_ref, u_ref, uq_ref, root_ref, rootq_ref, inner_ref, mean_ref, *, n_loc):
    q, ch = quarter_ref.shape
    first, second = [], []
    for ref in (sent_ref, other_ref):
        small = ref[q:, :].astype(F32)
        for r in range(4):
            block = small[16 * r : 16 * r + 16]
            both = block[0:2] + block[2:4] + block[4:6]
            first.append(both[0:1])
            second.append(both[1:2])
    sum_z, sum_g = jnp.concatenate(first), jnp.concatenate(second)
    mean_z = jnp.sum(sum_z, axis=0, keepdims=True) * (1.0 / (8 * n_loc))
    mean_g = jnp.sum(sum_g, axis=0, keepdims=True) * (1.0 / (8 * n_loc))
    dev_z = sum_z - n_loc * mean_z
    dev_g = sum_g * (1.0 / n_loc)
    turned = dot3(jnp.concatenate([dev_g, dev_z]), u_ref[...], 1, 0)
    turned_q = dot3(jnp.concatenate([dev_z, dev_g]), uq_ref[...], 1, 0)
    total = quarter_ref[...] + other_ref[:q, :].astype(F32) + 0.5 * dot3(turned_q, turned, 0, 0)
    root, rootq = root_ref[...], rootq_ref[...]
    inner = bf(total * (-1.0 / (rootq * root * (rootq + root))))
    for r in range(4):
        inner_ref[r] = inner
    mean_ref[...] = jnp.concatenate([mean_z, mean_g, jnp.zeros((6, ch), F32)])


def quarter_terms(got):
    ch = got.shape[2]
    q = ch // 4
    return pl.pallas_call(
        quarter_kernel,
        out_shape=(pltpu.HBM((q, ch), F32), pltpu.HBM((q + 64, ch), BF16)),
        compiler_params=params(8),
    )(*hbm(got))


def inner_terms(quarter, sent, other, eigvec, root, y, n_loc):
    q, ch = quarter.shape
    full = lambda *shape: pl.BlockSpec(shape, lambda i, y: (0,) * len(shape))
    return pl.pallas_call(
        functools.partial(inner_kernel, n_loc=n_loc),
        out_shape=(pltpu.HBM((4, q, ch), BF16), pltpu.HBM((8, ch), F32)),
        grid_spec=pltpu.PrefetchScalarGridSpec(
            num_scalar_prefetch=1,
            grid=(1,),
            in_specs=[
                full(q, ch),
                full(q + 64, ch),
                full(q + 64, ch),
                full(ch, ch),
                pl.BlockSpec((ch, q), lambda i, y: (0, y[0])),
                full(1, ch),
                pl.BlockSpec((q, 1), lambda i, y: (y[0], 0)),
            ],
            out_specs=(full(4, q, ch), full(8, ch)),
        ),
        compiler_params=params(16),
    )(y.reshape(1), *hbm(quarter, sent, other, eigvec, eigvec), root[None, :], root[:, None])


def first_kernel(u_ref, root_ref, g_ref, wsum_ref, first_ref):
    u = u_ref[...]
    whiten = dot3(u / root_ref[...], u, 1, 1)
    wh, wl = halves(whiten)
    wsum_ref[...] = wh.astype(F32) + wl.astype(F32)
    g = g_ref[...]
    first_ref[...] = dot(g, wh, 1, 0) + dot(g, wl, 1, 0)


def first_terms(eigvec, root, embed_grad):
    n_loc, ch = embed_grad.shape
    return pl.pallas_call(
        first_kernel,
        out_shape=(pltpu.HBM((ch, ch), F32), pltpu.HBM((n_loc, ch), F32)),
        compiler_params=params(14),
        cost_estimate=cost(6 * ch**3 + 4 * n_loc * ch * ch, 6 * n_loc * ch + 8 * ch * ch),
    )(*hbm(eigvec), root[None, :], *hbm(embed_grad))


def grad_z_kernel(u_ref, inner_ref, z_ref, first_ref, wsum_ref, mean_ref, out_ref, turned_ref, *, scale):
    u, inner = u_ref[...], inner_ref[...]
    uh, ul = halves(u)
    back = dot(uh, inner, 1, 0) + dot(ul, inner, 1, 0)
    dsigma = dot3(back, u, 1, 1) * scale
    dh, dl = halves(dsigma)
    mean = mean_ref[...]
    bias = dot3(mean, wsum_ref[...], 1, 0)[1:2] + dot3(mean, dh.astype(F32) + dl.astype(F32), 1, 0)[0:1]
    z = z_ref[...]
    out = first_ref[...] + dot(z, dh, 1, 0) + dot(z, dl, 1, 0) - bias
    out_ref[...] = bf(out)
    turned_ref[...] = bf(out.T)


def grad_z_of(eigvec, inner, embed, first, wsum, means, rows):
    n_loc, ch = embed.shape
    return pl.pallas_call(
        functools.partial(grad_z_kernel, scale=2.0 / rows),
        out_shape=(pltpu.HBM((n_loc, ch), BF16), pltpu.HBM((ch, n_loc), BF16)),
        compiler_params=params(20),
        cost_estimate=cost(10 * ch**3 + 4 * n_loc * ch * ch, 8 * n_loc * ch + 10 * ch * ch),
    )(*hbm(eigvec, inner, embed, first, wsum), means)


def ring_shapes(rows, cols):
    half = rows // 2
    return (
        pltpu.HBM((rows, cols), BF16),
        pltpu.HBM((rows, cols), BF16),
        pltpu.HBM((rows, cols), F32),
        pltpu.HBM((half, cols), F32),
        pltpu.HBM((half, cols), F32),
    )


def ring_store(r, start, acc, up_ref, down_ref, b0_ref, b1_ref, b3_ref, cols=slice(None)):
    size, half = acc.shape[0], b1_ref.shape[0]
    lower = start < half
    at = pl.ds(start % half, size)
    later = pl.ds(half + start % half, size)

    @pl.when(r == 0)
    def _():
        b0_ref[pl.ds(start, size), cols] = acc

    @pl.when(r == 1)
    def _():
        if lower:
            b1_ref[at, cols] = acc
        else:
            up_ref[at, cols] = bf(acc)

    @pl.when(r == 2)
    def _():
        if lower:
            up_ref[later, cols] = bf(acc)
        else:
            down_ref[at, cols] = bf(acc)

    @pl.when(r == 3)
    def _():
        if lower:
            down_ref[later, cols] = bf(acc)
        else:
            b3_ref[at, cols] = acc


def order_kernel(idx_ref, own_ref, right_ref, two_a_ref, two_b_ref, left_ref, out_ref, sems):
    fs = own_ref.shape[2]
    for g in range(8):
        place, side = idx_ref[g] // 2, idx_ref[g] % 2
        to, sem = out_ref.at[:, g * fs : (g + 1) * fs], sems.at[g]
        for n, ref in ((0, own_ref), (1, right_ref), (3, left_ref)):

            @pl.when(place == n)
            def _():
                pltpu.make_async_copy(ref.at[side], to, sem).start()

        for n, ref in ((0, two_a_ref), (1, two_b_ref)):

            @pl.when((place == 2) & (side == n))
            def _():
                pltpu.make_async_copy(ref.at[0], to, sem).start()

    for g in range(8):
        to, sem = out_ref.at[:, g * fs : (g + 1) * fs], sems.at[g]
        pltpu.make_async_copy(own_ref.at[0], to, sem).wait()


def in_order(sources, order):
    _, depth, fs = sources[0].shape
    return pl.pallas_call(
        order_kernel,
        out_shape=jax.ShapeDtypeStruct((depth, 8 * fs), BF16),
        in_specs=[pl.BlockSpec(memory_space=pltpu.SMEM)] + [pl.BlockSpec(memory_space=pl.ANY)] * 5,
        out_specs=pl.BlockSpec(memory_space=pl.ANY),
        scratch_shapes=[pltpu.SemaphoreType.DMA((8,))],
        compiler_params=params(4),
    )(order, *sources)


def stack_kernel(*refs):
    *sources, out_ref = refs
    at = 0
    for ref in sources:
        out_ref[at : at + ref.shape[0], :] = ref[...]
        at += ref.shape[0]


def stacked(sources):
    rows = sum(a.shape[0] for a in sources)
    return pl.pallas_call(
        stack_kernel,
        out_shape=pltpu.HBM((rows, sources[0].shape[1]), BF16),
        compiler_params=params(12),
    )(*sources)


def halves_kernel(core_ref, keep_in, give_in, keep_ref, give_ref):
    keep_ref[...] = bf(keep_in[...].astype(F32).T)
    give_ref[...] = bf(give_in[...].astype(F32).T)


def turned_halves(weight, core):
    rows, ch = weight.shape
    half = rows // 2
    shape = jax.ShapeDtypeStruct((ch, half), BF16)
    return pl.pallas_call(
        halves_kernel,
        out_shape=(shape, shape),
        grid_spec=pltpu.PrefetchScalarGridSpec(
            num_scalar_prefetch=1,
            grid=(1,),
            in_specs=[
                pl.BlockSpec((half, ch), lambda i, c: (c[0], 0)),
                pl.BlockSpec((half, ch), lambda i, c: (1 - c[0], 0)),
            ],
            out_specs=tuple(pl.BlockSpec((ch, half), lambda i, c: (0, 0)) for _ in range(2)),
        ),
        compiler_params=params(12),
    )(core.reshape(1), weight, weight)


def hidden_kernel(*refs):
    *lhs, w_ref, out_ref = refs
    _, rows, wide = out_ref.shape
    tile = rows // 2
    for start in range(0, rows, tile):
        acc, k0, seen = None, 0, 0
        for ref in lhs:
            depth = ref.shape[1]
            if seen <= start < seen + ref.shape[0]:
                term = dot(ref[start - seen : start - seen + tile, :], w_ref[k0 : k0 + depth, :], 1, 0)
                acc = term if acc is None else acc + term
            seen += ref.shape[0]
            if seen == rows:
                seen, k0 = 0, k0 + depth
        for r in range(4):
            out_ref[r, start : start + tile, :] = bf(acc[:, r * wide : (r + 1) * wide])


def hidden_terms(pieces, w_all):
    rows = pieces[0].shape[0]
    depth, wide = w_all.shape
    return pl.pallas_call(
        hidden_kernel,
        out_shape=pltpu.HBM((4, rows, wide // 4), BF16),
        compiler_params=params(20),
        cost_estimate=cost(2 * rows * wide * depth, 2 * (rows + wide) * depth + 2 * rows * wide),
    )(*pieces, w_all)


def here_kernel(idx_ref, p_ref, own_ref, out_ref):
    out_ref[...] = dot(p_ref[...], own_ref[...], 1, 0)


def weight_here(turned, hidden, order):
    ch, n_loc = turned.shape
    feat = hidden.shape[1] // 8
    return pl.pallas_call(
        here_kernel,
        out_shape=pltpu.HBM((ch, 4 * feat), F32),
        grid_spec=pltpu.PrefetchScalarGridSpec(
            num_scalar_prefetch=1,
            grid=(4,),
            in_specs=[
                pl.BlockSpec((ch, n_loc), lambda r, idx: (0, 0)),
                pl.BlockSpec((n_loc, feat), lambda r, idx: (0, idx[r])),
            ],
            out_specs=pl.BlockSpec((ch, feat), lambda r, idx: (0, r)),
        ),
        compiler_params=params(14),
        cost_estimate=cost(8 * ch * n_loc * feat, 8 * feat * (n_loc + 2 * ch)),
    )(order, *hbm(turned, hidden))


def weight_kernel(idx_ref, q_ref, own_ref, hx_ref, hk_ref, up_ref, down_ref, b0_ref, b1_ref, b3_ref, turned_ref):
    r = pl.program_id(0)
    core, x = idx_ref[4], idx_ref[5]
    half = hx_ref.shape[0]
    h = b1_ref.shape[0]
    sub = half // 4

    @pl.when(r == 0)
    def _():
        for n in range(8):
            k = core if n < 4 else 1 - core
            row = pl.multiple_of((k * 4 + (x + n) % 4) * sub, sub)
            turned_ref[:, n * sub : (n + 1) * sub] = bf(q_ref[pl.ds(row, sub), :].astype(F32).T)

    acc = own_ref[...] + dot(turned_ref[:, :half], hx_ref[...], 1, 0) + dot(turned_ref[:, half:], hk_ref[...], 1, 0)
    for start in (0, h):
        ring_store(r, start, acc[start : start + h], up_ref, down_ref, b0_ref, b1_ref, b3_ref)


def weight_terms(q_own, w_here, h_x, h_k, order):
    n_loc, ch = q_own.shape
    feat = h_x.shape[1] // 4
    shapes = ring_shapes(ch, feat)
    whole = lambda a: pl.BlockSpec(a.shape, lambda r, idx: (0, 0))
    return pl.pallas_call(
        weight_kernel,
        out_shape=shapes,
        grid_spec=pltpu.PrefetchScalarGridSpec(
            num_scalar_prefetch=1,
            grid=(4,),
            in_specs=[
                whole(q_own),
                pl.BlockSpec((ch, feat), lambda r, idx: (0, r)),
                pl.BlockSpec((n_loc // 2, feat), lambda r, idx: (0, r)),
                pl.BlockSpec((n_loc // 2, feat), lambda r, idx: (0, r)),
            ],
            out_specs=tuple(whole(a) for a in shapes),
            scratch_shapes=[pltpu.VMEM((ch, n_loc), BF16)],
        ),
        compiler_params=params(30),
        cost_estimate=cost(8 * n_loc * feat * ch, 8 * n_loc * feat + 28 * ch * feat),
    )(order, q_own, *hbm(w_here, h_x, h_k))


def ring_finish(terms, first, up, down):
    _, _, b0, b1, b3 = terms
    from_down, from_up = first
    h = b1.shape[0]
    from_down2 = up(bf(b1 + from_down[h:].astype(F32)))
    from_up2 = down(bf(b3 + from_up[:h].astype(F32)))
    lower = b0[:h] + from_up[h:].astype(F32) + from_down2.astype(F32)
    upper = b0[h:] + from_down[:h].astype(F32) + from_up2.astype(F32)
    return jnp.concatenate([lower, upper])


def local(hidden, weight, embed, embed_grad, eigvec, eigval):
    dp, chan = lax.axis_index("dp"), lax.axis_index("chan")
    zlo, y = dp // 4, dp % 4
    x, zhi, core = chan // 4, (chan // 2) % 2, chan % 2
    z = zhi * 2 + zlo
    n_loc = embed.shape[0]
    rows = n_loc * 8
    ch = embed.shape[1]
    feat = hidden.shape[1] // 8
    sub = n_loc // 8

    groups = [[0, 1, 2, 3], [4, 5, 6, 7]]
    x_groups = [[(i * 2 + a) * 2 + b for i in range(4)] for a in range(2) for b in range(2)]
    fs = weight.shape[0] // 8
    w_keep, w_give = turned_halves(weight, core)
    w_got = swap(w_give)
    wz = [
        jnp.concatenate([lax.dynamic_slice(a, (0, (z ^ j) * fs), (ch, fs)) for a in (w_keep, w_got)]) for j in range(4)
    ]
    message, hidden, *wz = tie(moments(embed, embed_grad, eigvec), hidden, *wz)
    got = lax.all_to_all(message, "dp", 0, 0, axis_index_groups=groups)

    def hidden_part(r, half, start, size):
        return lax.dynamic_slice(hidden, (start, (half * 4 + (y + r) % 4) * feat), (size, feat))

    mine = jnp.concatenate([hidden_part(r, 1 - zlo, (core * 4 + x) * sub, sub) for r in range(4)], axis=1)
    h0 = stacked([z_up(mine[: sub // 2]), z_down(mine[sub // 2 :])])
    h_left, h_right = x_up(h0), x_down(h0)
    wz = [wz[0]] + [z_flip[j](wz[j]) for j in (1, 2, 3)]
    quarter, sent = quarter_terms(got)
    other = z_flip[1](sent)
    root = jnp.sqrt(eigval)
    root, _ = tie(root, quarter)
    wsum, first = first_terms(eigvec, root, embed_grad)
    other, first, wsum, *wz = tie(other, first, wsum, *wz)
    w_own = jnp.stack([jnp.concatenate([wz[0], wz[2]]), jnp.concatenate([wz[1], wz[3]])])
    w_left, w_right = y_up(w_own), y_down(w_own)
    inner4, means = inner_terms(quarter, sent, other, eigvec, root, y, n_loc)
    inner = lax.all_to_all(inner4, "dp", 0, 0, axis_index_groups=groups).reshape(ch, ch)
    inner, h_left, h_right = tie(inner, h_left, h_right)
    h_two = x_up(h_left)
    grad_z, turned = grad_z_of(eigvec, inner, embed, first, wsum, means, rows)

    w_order = []
    for r in range(4):
        for f in range(2):
            y_s = 2 * (r % 2) + (zhi ^ f)
            w_order.append(((y_s - y) % 4) * 2 + ((r // 2) ^ zlo))
    w_order = jnp.stack(w_order).astype(jnp.int32)
    h_order = jnp.stack([zlo * 4 + (y + r) % 4 for r in range(4)] + [core, x]).astype(jnp.int32)

    ht = n_loc // 2
    r_own = z_flip[1](grad_z)
    r_oth = z_flip[3](grad_z)
    own2 = swap(grad_z)
    turned, w_left, w_right = tie(turned, w_left, w_right)
    w_here = weight_here(turned, hidden, h_order)
    w_two = y_up(w_left[:1]), y_down(w_right[1:])
    w_all = in_order([w_own, w_right, *w_two, w_left], w_order)
    h_x = stacked([h0, h_right, h_two, h_left])
    r_own, r_oth, w_here, w_all, h_x = tie(r_own, r_oth, w_here, w_all, h_x)

    far = z_flip[1](r_oth[:ht]), z_flip[3](r_own[ht:])
    par = hidden_terms([r_own, swap(r_own), r_oth, swap(r_oth)], w_all)
    _, h_x = tie(par, h_x)
    h_k = swap(h_x)
    par_got = lax.all_to_all(par, "chan", 0, 0, axis_index_groups=x_groups)

    r_own, _ = tie(r_own, par)
    w_terms = weight_terms(r_own, w_here, h_x, h_k, h_order)
    w_first = y_up(w_terms[0]), y_down(w_terms[1])

    grad_z, _, *far = tie(grad_z, w_terms[0], *far)
    far2 = [swap(a) for a in far]
    own = hidden_terms([grad_z, own2, *far, *far2], w_all)
    own, par_got = tie(own, par_got)
    own_got = lax.all_to_all(own, "chan", 0, 0, axis_index_groups=x_groups)
    s_par = bf(jnp.sum(par_got.astype(F32), axis=0))
    p1 = z_flip[1](s_par[:, :fs])
    p3 = z_flip[3](s_par[:, fs:])
    w_sum = ring_finish(w_terms, w_first, y_up, y_down)
    s_own = bf(jnp.sum(own_got.astype(F32), axis=0))
    p0 = s_own[:, :fs]
    p2 = z_flip[2](s_own[:, fs:])
    grad_weight = bf(w_sum.T)
    odd = zlo == 1
    u0, u1 = jnp.where(odd, p1, p0), jnp.where(odd, p0, p1)
    u2, u3 = jnp.where(odd, p3, p2), jnp.where(odd, p2, p3)
    low = jnp.concatenate([u0, u1], axis=1)
    high = jnp.concatenate([u2, u3], axis=1)
    up = zhi == 1
    grad_hidden = jnp.concatenate([jnp.where(up, high, low), jnp.where(up, low, high)], axis=1)
    return grad_weight, grad_hidden


def solution(mesh):
    in_specs = (
        P("dp", None),
        P("dp", "chan"),
        P("dp", "chan"),
        P("dp", "chan"),
        P("chan", None),
        P("chan"),
    )
    out_specs = (P("dp", "chan"), P("dp", "chan"))
    return jax.shard_map(local, mesh=mesh, in_specs=in_specs, out_specs=out_specs, check_vma=False)
```

```python
import functools

import jax
import jax.numpy as jnp
from jax import lax
from jax.experimental import pallas as pl
from jax.experimental.pallas import tpu as pltpu
from jax.sharding import PartitionSpec as P

F32 = jnp.float32
BF16 = jnp.bfloat16
AXES = ("dp", "chan")


def place_of(index):
    dp, chan = divmod(index, 16)
    zlo, y = divmod(dp, 4)
    x, rest = divmod(chan, 4)
    zhi, core = divmod(rest, 2)
    return x, y, zhi * 2 + zlo, core


def index_of(x, y, z, core):
    zhi, zlo = divmod(z % 4, 2)
    return (zlo * 4 + y % 4) * 16 + ((x % 4) * 2 + zhi) * 2 + core


def mover(step):
    pairs = [(i, index_of(*step(*place_of(i)))) for i in range(128)]
    return lambda a: lax.ppermute(a, AXES, pairs)


x_up = mover(lambda x, y, z, k: (x + 1, y, z, k))
x_down = mover(lambda x, y, z, k: (x - 1, y, z, k))
y_up = mover(lambda x, y, z, k: (x, y + 1, z, k))
y_down = mover(lambda x, y, z, k: (x, y - 1, z, k))
z_up = mover(lambda x, y, z, k: (x, y, z + 1, k))
z_down = mover(lambda x, y, z, k: (x, y, z - 1, k))
z_flip = [None] + [mover(lambda x, y, z, k, j=j: (x, y, z ^ j, k)) for j in (1, 2, 3)]
swap = mover(lambda x, y, z, k: (x, y, z, 1 - k))


def bf(a):
    return a.astype(BF16)


def tie(*arrays):
    return lax.optimization_barrier(arrays)


def halves(a):
    head = bf(a)
    return head, bf(a - head.astype(F32))


def dot(a, b, ca, cb):
    return lax.dot_general(a, b, (((ca,), (cb,)), ((), ())), preferred_element_type=F32)


def dot3(a, b, ca, cb):
    (ah, al), (bh, bl) = halves(a), halves(b)
    return dot(ah, bh, ca, cb) + (dot(ah, bl, ca, cb) + dot(al, bh, ca, cb))


def hbm(*arrays):
    return [pltpu.with_memory_space_constraint(a, pltpu.HBM) for a in arrays]


def params(mib):
    return pltpu.CompilerParams(vmem_limit_bytes=mib * 2**20)


def cost(flops, nbytes):
    return pl.CostEstimate(flops=int(flops), bytes_accessed=int(nbytes), transcendentals=0)


def moments_kernel(z_ref, g_ref, u_ref, out_ref):
    n_loc, ch = z_ref.shape
    q = ch // 4
    z, g = z_ref[...], g_ref[...]
    sum_z = jnp.sum(z.astype(F32), axis=0, keepdims=True)
    sum_g = jnp.sum(g.astype(F32), axis=0, keepdims=True)
    zero = jnp.zeros((7, ch), F32)
    outer = dot3(jnp.concatenate([sum_z * (1.0 / n_loc), zero]), jnp.concatenate([sum_g, zero]), 0, 0)
    part = dot(z, g, 0, 0) - outer
    sym = 0.5 * (part + part.T)
    u = u_ref[...]
    rotated = dot3(dot3(u, sym, 0, 0), u, 1, 0)
    sums = jnp.concatenate([sum_z, sum_g])
    parts = []
    for _ in range(3):
        head = bf(sums).astype(F32)
        parts.append(head)
        sums = sums - head
    small = bf(jnp.concatenate(parts + [jnp.zeros((10, ch), F32)]))
    for r in range(4):
        out_ref[r, :q, :] = bf(rotated[r * q : (r + 1) * q])
        out_ref[r, q:, :] = small


def moments(embed, embed_grad, eigvec):
    n_loc, ch = embed.shape
    return pl.pallas_call(
        moments_kernel,
        out_shape=pltpu.HBM((4, ch // 4 + 16, ch), BF16),
        compiler_params=params(20),
        cost_estimate=cost(2 * n_loc * ch * ch + 12 * ch**3, 4 * n_loc * ch + 6 * ch * ch),
    )(*hbm(embed, embed_grad, eigvec))


def quarter_kernel(got_ref, quarter_ref, sent_ref):
    q = quarter_ref.shape[0]
    total = sum(got_ref[r, :q, :].astype(F32) for r in range(4))
    quarter_ref[...] = total
    sent_ref[:q, :] = bf(total)
    for r in range(4):
        sent_ref[q + 16 * r : q + 16 * (r + 1), :] = got_ref[r, q:, :]


def inner_kernel(y_ref, quarter_ref, sent_ref, other_ref, u_ref, uq_ref, root_ref, rootq_ref, inner_ref, mean_ref, *, n_loc):
    q, ch = quarter_ref.shape
    first, second = [], []
    for ref in (sent_ref, other_ref):
        small = ref[q:, :].astype(F32)
        for r in range(4):
            block = small[16 * r : 16 * r + 16]
            both = block[0:2] + block[2:4] + block[4:6]
            first.append(both[0:1])
            second.append(both[1:2])
    sum_z, sum_g = jnp.concatenate(first), jnp.concatenate(second)
    mean_z = jnp.sum(sum_z, axis=0, keepdims=True) * (1.0 / (8 * n_loc))
    mean_g = jnp.sum(sum_g, axis=0, keepdims=True) * (1.0 / (8 * n_loc))
    dev_z = sum_z - n_loc * mean_z
    dev_g = sum_g * (1.0 / n_loc)
    turned = dot3(jnp.concatenate([dev_g, dev_z]), u_ref[...], 1, 0)
    turned_q = dot3(jnp.concatenate([dev_z, dev_g]), uq_ref[...], 1, 0)
    total = quarter_ref[...] + other_ref[:q, :].astype(F32) + 0.5 * dot3(turned_q, turned, 0, 0)
    root, rootq = root_ref[...], rootq_ref[...]
    inner = bf(total * (-1.0 / (rootq * root * (rootq + root))))
    for r in range(4):
        inner_ref[r] = inner
    mean_ref[...] = jnp.concatenate([mean_z, mean_g, jnp.zeros((6, ch), F32)])


def quarter_terms(got):
    ch = got.shape[2]
    q = ch // 4
    return pl.pallas_call(
        quarter_kernel,
        out_shape=(pltpu.HBM((q, ch), F32), pltpu.HBM((q + 64, ch), BF16)),
        compiler_params=params(8),
    )(*hbm(got))


def inner_terms(quarter, sent, other, eigvec, root, y, n_loc):
    q, ch = quarter.shape
    full = lambda *shape: pl.BlockSpec(shape, lambda i, y: (0,) * len(shape))
    return pl.pallas_call(
        functools.partial(inner_kernel, n_loc=n_loc),
        out_shape=(pltpu.HBM((4, q, ch), BF16), pltpu.HBM((8, ch), F32)),
        grid_spec=pltpu.PrefetchScalarGridSpec(
            num_scalar_prefetch=1,
            grid=(1,),
            in_specs=[
                full(q, ch),
                full(q + 64, ch),
                full(q + 64, ch),
                full(ch, ch),
                pl.BlockSpec((ch, q), lambda i, y: (0, y[0])),
                full(1, ch),
                pl.BlockSpec((q, 1), lambda i, y: (y[0], 0)),
            ],
            out_specs=(full(4, q, ch), full(8, ch)),
        ),
        compiler_params=params(16),
    )(y.reshape(1), *hbm(quarter, sent, other, eigvec, eigvec), root[None, :], root[:, None])


def first_kernel(u_ref, root_ref, g_ref, wsum_ref, first_ref):
    u = u_ref[...]
    whiten = dot3(u / root_ref[...], u, 1, 1)
    wh, wl = halves(whiten)
    wsum_ref[...] = wh.astype(F32) + wl.astype(F32)
    g = g_ref[...]
    first_ref[...] = dot(g, wh, 1, 0) + dot(g, wl, 1, 0)


def first_terms(eigvec, root, embed_grad):
    n_loc, ch = embed_grad.shape
    return pl.pallas_call(
        first_kernel,
        out_shape=(pltpu.HBM((ch, ch), F32), pltpu.HBM((n_loc, ch), F32)),
        compiler_params=params(14),
        cost_estimate=cost(6 * ch**3 + 4 * n_loc * ch * ch, 6 * n_loc * ch + 8 * ch * ch),
    )(*hbm(eigvec), root[None, :], *hbm(embed_grad))


def grad_z_kernel(u_ref, inner_ref, z_ref, first_ref, wsum_ref, mean_ref, out_ref, turned_ref, *, scale):
    u, inner = u_ref[...], inner_ref[...]
    uh, ul = halves(u)
    back = dot(uh, inner, 1, 0) + dot(ul, inner, 1, 0)
    dsigma = dot3(back, u, 1, 1) * scale
    dh, dl = halves(dsigma)
    mean = mean_ref[...]
    bias = dot3(mean, wsum_ref[...], 1, 0)[1:2] + dot3(mean, dh.astype(F32) + dl.astype(F32), 1, 0)[0:1]
    z = z_ref[...]
    out = first_ref[...] + dot(z, dh, 1, 0) + dot(z, dl, 1, 0) - bias
    out_ref[...] = bf(out)
    turned_ref[...] = bf(out.T)


def grad_z_of(eigvec, inner, embed, first, wsum, means, rows):
    n_loc, ch = embed.shape
    return pl.pallas_call(
        functools.partial(grad_z_kernel, scale=2.0 / rows),
        out_shape=(pltpu.HBM((n_loc, ch), BF16), pltpu.HBM((ch, n_loc), BF16)),
        compiler_params=params(20),
        cost_estimate=cost(10 * ch**3 + 4 * n_loc * ch * ch, 8 * n_loc * ch + 10 * ch * ch),
    )(*hbm(eigvec, inner, embed, first, wsum), means)


def ring_shapes(rows, cols):
    half = rows // 2
    return (
        pltpu.HBM((rows, cols), BF16),
        pltpu.HBM((rows, cols), BF16),
        pltpu.HBM((rows, cols), F32),
        pltpu.HBM((half, cols), F32),
        pltpu.HBM((half, cols), F32),
    )


def ring_store(r, start, acc, up_ref, down_ref, b0_ref, b1_ref, b3_ref, cols=slice(None)):
    size, half = acc.shape[0], b1_ref.shape[0]
    lower = start < half
    at = pl.ds(start % half, size)
    later = pl.ds(half + start % half, size)

    @pl.when(r == 0)
    def _():
        b0_ref[pl.ds(start, size), cols] = acc

    @pl.when(r == 1)
    def _():
        if lower:
            b1_ref[at, cols] = acc
        else:
            up_ref[at, cols] = bf(acc)

    @pl.when(r == 2)
    def _():
        if lower:
            up_ref[later, cols] = bf(acc)
        else:
            down_ref[at, cols] = bf(acc)

    @pl.when(r == 3)
    def _():
        if lower:
            down_ref[later, cols] = bf(acc)
        else:
            b3_ref[at, cols] = acc


def order_kernel(idx_ref, own_ref, right_ref, two_a_ref, two_b_ref, left_ref, out_ref, sems):
    fs = own_ref.shape[2]
    for g in range(8):
        place, side = idx_ref[g] // 2, idx_ref[g] % 2
        to, sem = out_ref.at[:, g * fs : (g + 1) * fs], sems.at[g]
        for n, ref in ((0, own_ref), (1, right_ref), (3, left_ref)):

            @pl.when(place == n)
            def _():
                pltpu.make_async_copy(ref.at[side], to, sem).start()

        for n, ref in ((0, two_a_ref), (1, two_b_ref)):

            @pl.when((place == 2) & (side == n))
            def _():
                pltpu.make_async_copy(ref.at[0], to, sem).start()

    for g in range(8):
        to, sem = out_ref.at[:, g * fs : (g + 1) * fs], sems.at[g]
        pltpu.make_async_copy(own_ref.at[0], to, sem).wait()


def in_order(sources, order):
    _, depth, fs = sources[0].shape
    return pl.pallas_call(
        order_kernel,
        out_shape=jax.ShapeDtypeStruct((depth, 8 * fs), BF16),
        in_specs=[pl.BlockSpec(memory_space=pltpu.SMEM)] + [pl.BlockSpec(memory_space=pl.ANY)] * 5,
        out_specs=pl.BlockSpec(memory_space=pl.ANY),
        scratch_shapes=[pltpu.SemaphoreType.DMA((8,))],
        compiler_params=params(4),
    )(order, *sources)


def stack_kernel(*refs):
    *sources, out_ref = refs
    at = 0
    for ref in sources:
        out_ref[at : at + ref.shape[0], :] = ref[...]
        at += ref.shape[0]


def stacked(sources):
    rows = sum(a.shape[0] for a in sources)
    return pl.pallas_call(
        stack_kernel,
        out_shape=pltpu.HBM((rows, sources[0].shape[1]), BF16),
        compiler_params=params(12),
    )(*sources)


def halves_kernel(core_ref, keep_in, give_in, keep_ref, give_ref):
    keep_ref[...] = bf(keep_in[...].astype(F32).T)
    give_ref[...] = bf(give_in[...].astype(F32).T)


def turned_halves(weight, core):
    rows, ch = weight.shape
    half = rows // 2
    shape = jax.ShapeDtypeStruct((ch, half), BF16)
    return pl.pallas_call(
        halves_kernel,
        out_shape=(shape, shape),
        grid_spec=pltpu.PrefetchScalarGridSpec(
            num_scalar_prefetch=1,
            grid=(1,),
            in_specs=[
                pl.BlockSpec((half, ch), lambda i, c: (c[0], 0)),
                pl.BlockSpec((half, ch), lambda i, c: (1 - c[0], 0)),
            ],
            out_specs=tuple(pl.BlockSpec((ch, half), lambda i, c: (0, 0)) for _ in range(2)),
        ),
        compiler_params=params(12),
    )(core.reshape(1), weight, weight)


def hidden_kernel(*refs):
    *lhs, w_ref, out_ref = refs
    _, rows, wide = out_ref.shape
    tile = rows // 2
    for start in range(0, rows, tile):
        acc, k0, seen = None, 0, 0
        for ref in lhs:
            depth = ref.shape[1]
            if seen <= start < seen + ref.shape[0]:
                term = dot(ref[start - seen : start - seen + tile, :], w_ref[k0 : k0 + depth, :], 1, 0)
                acc = term if acc is None else acc + term
            seen += ref.shape[0]
            if seen == rows:
                seen, k0 = 0, k0 + depth
        for r in range(4):
            out_ref[r, start : start + tile, :] = bf(acc[:, r * wide : (r + 1) * wide])


def hidden_terms(pieces, w_all):
    rows = pieces[0].shape[0]
    depth, wide = w_all.shape
    return pl.pallas_call(
        hidden_kernel,
        out_shape=pltpu.HBM((4, rows, wide // 4), BF16),
        compiler_params=params(20),
        cost_estimate=cost(2 * rows * wide * depth, 2 * (rows + wide) * depth + 2 * rows * wide),
    )(*pieces, w_all)


def here_kernel(idx_ref, p_ref, own_ref, out_ref):
    out_ref[...] = dot(p_ref[...], own_ref[...], 1, 0)


def weight_here(turned, hidden, order):
    ch, n_loc = turned.shape
    feat = hidden.shape[1] // 8
    return pl.pallas_call(
        here_kernel,
        out_shape=pltpu.HBM((ch, 4 * feat), F32),
        grid_spec=pltpu.PrefetchScalarGridSpec(
            num_scalar_prefetch=1,
            grid=(4,),
            in_specs=[
                pl.BlockSpec((ch, n_loc), lambda r, idx: (0, 0)),
                pl.BlockSpec((n_loc, feat), lambda r, idx: (0, idx[r])),
            ],
            out_specs=pl.BlockSpec((ch, feat), lambda r, idx: (0, r)),
        ),
        compiler_params=params(14),
        cost_estimate=cost(8 * ch * n_loc * feat, 8 * feat * (n_loc + 2 * ch)),
    )(order, *hbm(turned, hidden))


def weight_kernel(idx_ref, q_ref, own_ref, hx_ref, hk_ref, up_ref, down_ref, b0_ref, b1_ref, b3_ref, turned_ref):
    r = pl.program_id(0)
    core, x = idx_ref[4], idx_ref[5]
    half = hx_ref.shape[0]
    h = b1_ref.shape[0]
    sub = half // 4

    @pl.when(r == 0)
    def _():
        for n in range(8):
            k = core if n < 4 else 1 - core
            row = pl.multiple_of((k * 4 + (x + n) % 4) * sub, sub)
            turned_ref[:, n * sub : (n + 1) * sub] = bf(q_ref[pl.ds(row, sub), :].astype(F32).T)

    acc = own_ref[...] + dot(turned_ref[:, :half], hx_ref[...], 1, 0) + dot(turned_ref[:, half:], hk_ref[...], 1, 0)
    for start in (0, h):
        ring_store(r, start, acc[start : start + h], up_ref, down_ref, b0_ref, b1_ref, b3_ref)


def weight_terms(q_own, w_here, h_x, h_k, order):
    n_loc, ch = q_own.shape
    feat = h_x.shape[1] // 4
    shapes = ring_shapes(ch, feat)
    whole = lambda a: pl.BlockSpec(a.shape, lambda r, idx: (0, 0))
    return pl.pallas_call(
        weight_kernel,
        out_shape=shapes,
        grid_spec=pltpu.PrefetchScalarGridSpec(
            num_scalar_prefetch=1,
            grid=(4,),
            in_specs=[
                whole(q_own),
                pl.BlockSpec((ch, feat), lambda r, idx: (0, r)),
                pl.BlockSpec((n_loc // 2, feat), lambda r, idx: (0, r)),
                pl.BlockSpec((n_loc // 2, feat), lambda r, idx: (0, r)),
            ],
            out_specs=tuple(whole(a) for a in shapes),
            scratch_shapes=[pltpu.VMEM((ch, n_loc), BF16)],
        ),
        compiler_params=params(30),
        cost_estimate=cost(8 * n_loc * feat * ch, 8 * n_loc * feat + 28 * ch * feat),
    )(order, q_own, *hbm(w_here, h_x, h_k))


def finish_kernel(b0_ref, down_ref, up_ref, down2_ref, up2_ref, out_ref):
    h = down2_ref.shape[0]
    lower = b0_ref[:h, :] + up_ref[h:, :].astype(F32) + down2_ref[...].astype(F32)
    upper = b0_ref[h:, :] + down_ref[:h, :].astype(F32) + up2_ref[...].astype(F32)
    out_ref[:, :h] = bf(lower.T)
    out_ref[:, h:] = bf(upper.T)


def ring_finish(terms, first, up, down):
    _, _, b0, b1, b3 = terms
    from_down, from_up = first
    h = b1.shape[0]
    from_down2 = up(bf(b1 + from_down[h:].astype(F32)))
    from_up2 = down(bf(b3 + from_up[:h].astype(F32)))
    return pl.pallas_call(
        finish_kernel,
        out_shape=jax.ShapeDtypeStruct(b0.shape[::-1], BF16),
        compiler_params=params(16),
    )(*hbm(b0, from_down, from_up), from_down2, from_up2)


def placed_kernel(z_ref, *refs):
    *pieces, out_ref = refs
    for j, ref in enumerate(pieces):
        wide = ref.shape[1]
        out_ref[:, pl.ds(pl.multiple_of((z_ref[0] ^ j) * wide, wide), wide)] = ref[...]


def placed(pieces, z):
    rows, wide = pieces[0].shape
    return pl.pallas_call(
        placed_kernel,
        out_shape=jax.ShapeDtypeStruct((rows, 4 * wide), BF16),
        in_specs=[pl.BlockSpec(memory_space=pltpu.SMEM)] + [pl.BlockSpec(memory_space=pltpu.VMEM)] * 4,
        compiler_params=params(8),
    )(z.reshape(1), *pieces)


def local(hidden, weight, embed, embed_grad, eigvec, eigval):
    dp, chan = lax.axis_index("dp"), lax.axis_index("chan")
    zlo, y = dp // 4, dp % 4
    x, zhi, core = chan // 4, (chan // 2) % 2, chan % 2
    z = zhi * 2 + zlo
    n_loc = embed.shape[0]
    rows = n_loc * 8
    ch = embed.shape[1]
    feat = hidden.shape[1] // 8
    sub = n_loc // 8

    groups = [[0, 1, 2, 3], [4, 5, 6, 7]]
    x_groups = [[(i * 2 + a) * 2 + b for i in range(4)] for a in range(2) for b in range(2)]
    fs = weight.shape[0] // 8
    w_keep, w_give = turned_halves(weight, core)
    w_got = swap(w_give)
    wz = [
        jnp.concatenate([lax.dynamic_slice(a, (0, (z ^ j) * fs), (ch, fs)) for a in (w_keep, w_got)]) for j in range(4)
    ]
    message, hidden, *wz = tie(moments(embed, embed_grad, eigvec), hidden, *wz)
    got = lax.all_to_all(message, "dp", 0, 0, axis_index_groups=groups)

    def hidden_part(r, half, start, size):
        return lax.dynamic_slice(hidden, (start, (half * 4 + (y + r) % 4) * feat), (size, feat))

    mine = jnp.concatenate([hidden_part(r, 1 - zlo, (core * 4 + x) * sub, sub) for r in range(4)], axis=1)
    h0 = stacked([z_up(mine[: sub // 2]), z_down(mine[sub // 2 :])])
    h_left, h_right = x_up(h0), x_down(h0)
    wz = [wz[0]] + [z_flip[j](wz[j]) for j in (1, 2, 3)]
    quarter, sent = quarter_terms(got)
    other = z_flip[1](sent)
    root = jnp.sqrt(eigval)
    root, _ = tie(root, quarter)
    wsum, first = first_terms(eigvec, root, embed_grad)
    other, first, wsum, *wz = tie(other, first, wsum, *wz)
    w_own = jnp.stack([jnp.concatenate([wz[0], wz[2]]), jnp.concatenate([wz[1], wz[3]])])
    w_left, w_right = y_up(w_own), y_down(w_own)
    inner4, means = inner_terms(quarter, sent, other, eigvec, root, y, n_loc)
    inner = lax.all_to_all(inner4, "dp", 0, 0, axis_index_groups=groups).reshape(ch, ch)
    inner, h_left, h_right = tie(inner, h_left, h_right)
    h_two = x_up(h_left)
    grad_z, turned = grad_z_of(eigvec, inner, embed, first, wsum, means, rows)

    w_order = []
    for r in range(4):
        for f in range(2):
            y_s = 2 * (r % 2) + (zhi ^ f)
            w_order.append(((y_s - y) % 4) * 2 + ((r // 2) ^ zlo))
    w_order = jnp.stack(w_order).astype(jnp.int32)
    h_order = jnp.stack([zlo * 4 + (y + r) % 4 for r in range(4)] + [core, x]).astype(jnp.int32)

    ht = n_loc // 2
    r_own = z_flip[1](grad_z)
    r_oth = z_flip[3](grad_z)
    own2 = swap(grad_z)
    turned, w_left, w_right = tie(turned, w_left, w_right)
    w_here = weight_here(turned, hidden, h_order)
    w_two = y_up(w_left[:1]), y_down(w_right[1:])
    w_all = in_order([w_own, w_right, *w_two, w_left], w_order)
    h_x = stacked([h0, h_right, h_two, h_left])
    r_own, r_oth, w_here, w_all, h_x = tie(r_own, r_oth, w_here, w_all, h_x)

    far = z_flip[1](r_oth[:ht]), z_flip[3](r_own[ht:])
    par = hidden_terms([r_own, swap(r_own), r_oth, swap(r_oth)], w_all)
    _, h_x = tie(par, h_x)
    h_k = swap(h_x)
    par_got = lax.all_to_all(par, "chan", 0, 0, axis_index_groups=x_groups)

    r_own, _ = tie(r_own, par)
    w_terms = weight_terms(r_own, w_here, h_x, h_k, h_order)
    w_first = y_up(w_terms[0]), y_down(w_terms[1])

    grad_z, _, *far = tie(grad_z, w_terms[0], *far)
    far2 = [swap(a) for a in far]
    own = hidden_terms([grad_z, own2, *far, *far2], w_all)
    own, par_got = tie(own, par_got)
    own_got = lax.all_to_all(own, "chan", 0, 0, axis_index_groups=x_groups)
    s_par = bf(jnp.sum(par_got.astype(F32), axis=0))
    p1 = z_flip[1](s_par[:, :fs])
    p3 = z_flip[3](s_par[:, fs:])
    grad_weight = ring_finish(w_terms, w_first, y_up, y_down)
    s_own = bf(jnp.sum(own_got.astype(F32), axis=0))
    p0 = s_own[:, :fs]
    p2 = z_flip[2](s_own[:, fs:])
    grad_hidden = placed([p0, p1, p2, p3], z)
    return grad_weight, grad_hidden


def solution(mesh):
    in_specs = (
        P("dp", None),
        P("dp", "chan"),
        P("dp", "chan"),
        P("dp", "chan"),
        P("chan", None),
        P("chan"),
    )
    out_specs = (P("dp", "chan"), P("dp", "chan"))
    return jax.shard_map(local, mesh=mesh, in_specs=in_specs, out_specs=out_specs, check_vma=False)
```

```python
import functools

import jax
import jax.numpy as jnp
from jax import lax
from jax.experimental import pallas as pl
from jax.experimental.pallas import tpu as pltpu
from jax.sharding import PartitionSpec as P

F32 = jnp.float32
BF16 = jnp.bfloat16
AXES = ("dp", "chan")


def place_of(index):
    dp, chan = divmod(index, 16)
    zlo, y = divmod(dp, 4)
    x, rest = divmod(chan, 4)
    zhi, core = divmod(rest, 2)
    return x, y, zhi * 2 + zlo, core


def index_of(x, y, z, core):
    zhi, zlo = divmod(z % 4, 2)
    return (zlo * 4 + y % 4) * 16 + ((x % 4) * 2 + zhi) * 2 + core


def mover(step):
    pairs = [(i, index_of(*step(*place_of(i)))) for i in range(128)]
    return lambda a: lax.ppermute(a, AXES, pairs)


x_up = mover(lambda x, y, z, k: (x + 1, y, z, k))
x_down = mover(lambda x, y, z, k: (x - 1, y, z, k))
y_up = mover(lambda x, y, z, k: (x, y + 1, z, k))
y_down = mover(lambda x, y, z, k: (x, y - 1, z, k))
z_up = mover(lambda x, y, z, k: (x, y, z + 1, k))
z_down = mover(lambda x, y, z, k: (x, y, z - 1, k))
z_flip = [None] + [mover(lambda x, y, z, k, j=j: (x, y, z ^ j, k)) for j in (1, 2, 3)]
swap = mover(lambda x, y, z, k: (x, y, z, 1 - k))


def bf(a):
    return a.astype(BF16)


def tie(*arrays):
    return lax.optimization_barrier(arrays)


def halves(a):
    head = bf(a)
    return head, bf(a - head.astype(F32))


def dot(a, b, ca, cb):
    return lax.dot_general(a, b, (((ca,), (cb,)), ((), ())), preferred_element_type=F32)


def dot3(a, b, ca, cb):
    (ah, al), (bh, bl) = halves(a), halves(b)
    return dot(ah, bh, ca, cb) + (dot(ah, bl, ca, cb) + dot(al, bh, ca, cb))


def hbm(*arrays):
    return [pltpu.with_memory_space_constraint(a, pltpu.HBM) for a in arrays]


def params(mib):
    return pltpu.CompilerParams(vmem_limit_bytes=mib * 2**20)


def cost(flops, nbytes):
    return pl.CostEstimate(flops=int(flops), bytes_accessed=int(nbytes), transcendentals=0)


def moments_kernel(z_ref, g_ref, u_ref, out_ref):
    n_loc, ch = z_ref.shape
    q = ch // 4
    z, g = z_ref[...], g_ref[...]
    sum_z = jnp.sum(z.astype(F32), axis=0, keepdims=True)
    sum_g = jnp.sum(g.astype(F32), axis=0, keepdims=True)
    zero = jnp.zeros((7, ch), F32)
    outer = dot3(jnp.concatenate([sum_z * (1.0 / n_loc), zero]), jnp.concatenate([sum_g, zero]), 0, 0)
    part = dot(z, g, 0, 0) - outer
    sym = 0.5 * (part + part.T)
    u = u_ref[...]
    rotated = dot3(dot3(u, sym, 0, 0), u, 1, 0)
    sums = jnp.concatenate([sum_z, sum_g])
    parts = []
    for _ in range(3):
        head = bf(sums).astype(F32)
        parts.append(head)
        sums = sums - head
    small = bf(jnp.concatenate(parts + [jnp.zeros((10, ch), F32)]))
    for r in range(4):
        out_ref[r, :q, :] = bf(rotated[r * q : (r + 1) * q])
        out_ref[r, q:, :] = small


def moments(embed, embed_grad, eigvec):
    n_loc, ch = embed.shape
    return pl.pallas_call(
        moments_kernel,
        out_shape=pltpu.HBM((4, ch // 4 + 16, ch), BF16),
        compiler_params=params(20),
        cost_estimate=cost(2 * n_loc * ch * ch + 12 * ch**3, 4 * n_loc * ch + 6 * ch * ch),
    )(*hbm(embed, embed_grad, eigvec))


def quarter_kernel(got_ref, quarter_ref, sent_ref):
    q = quarter_ref.shape[0]
    total = sum(got_ref[r, :q, :].astype(F32) for r in range(4))
    quarter_ref[...] = total
    sent_ref[:q, :] = bf(total)
    for r in range(4):
        sent_ref[q + 16 * r : q + 16 * (r + 1), :] = got_ref[r, q:, :]


def inner_kernel(y_ref, quarter_ref, sent_ref, other_ref, u_ref, uq_ref, root_ref, rootq_ref, inner_ref, mean_ref, *, n_loc):
    q, ch = quarter_ref.shape
    first, second = [], []
    for ref in (sent_ref, other_ref):
        small = ref[q:, :].astype(F32)
        for r in range(4):
            block = small[16 * r : 16 * r + 16]
            both = block[0:2] + block[2:4] + block[4:6]
            first.append(both[0:1])
            second.append(both[1:2])
    sum_z, sum_g = jnp.concatenate(first), jnp.concatenate(second)
    mean_z = jnp.sum(sum_z, axis=0, keepdims=True) * (1.0 / (8 * n_loc))
    mean_g = jnp.sum(sum_g, axis=0, keepdims=True) * (1.0 / (8 * n_loc))
    dev_z = sum_z - n_loc * mean_z
    dev_g = sum_g * (1.0 / n_loc)
    turned = dot3(jnp.concatenate([dev_g, dev_z]), u_ref[...], 1, 0)
    turned_q = dot3(jnp.concatenate([dev_z, dev_g]), uq_ref[...], 1, 0)
    total = quarter_ref[...] + other_ref[:q, :].astype(F32) + 0.5 * dot3(turned_q, turned, 0, 0)
    root, rootq = root_ref[...], rootq_ref[...]
    inner = bf(total * (-1.0 / (rootq * root * (rootq + root))))
    for r in range(4):
        inner_ref[r] = inner
    mean_ref[...] = jnp.concatenate([mean_z, mean_g, jnp.zeros((6, ch), F32)])


def quarter_terms(got):
    ch = got.shape[2]
    q = ch // 4
    return pl.pallas_call(
        quarter_kernel,
        out_shape=(pltpu.HBM((q, ch), F32), pltpu.HBM((q + 64, ch), BF16)),
        compiler_params=params(8),
    )(*hbm(got))


def inner_terms(quarter, sent, other, eigvec, root, y, n_loc):
    q, ch = quarter.shape
    full = lambda *shape: pl.BlockSpec(shape, lambda i, y: (0,) * len(shape))
    return pl.pallas_call(
        functools.partial(inner_kernel, n_loc=n_loc),
        out_shape=(pltpu.HBM((4, q, ch), BF16), pltpu.HBM((8, ch), F32)),
        grid_spec=pltpu.PrefetchScalarGridSpec(
            num_scalar_prefetch=1,
            grid=(1,),
            in_specs=[
                full(q, ch),
                full(q + 64, ch),
                full(q + 64, ch),
                full(ch, ch),
                pl.BlockSpec((ch, q), lambda i, y: (0, y[0])),
                full(1, ch),
                pl.BlockSpec((q, 1), lambda i, y: (y[0], 0)),
            ],
            out_specs=(full(4, q, ch), full(8, ch)),
        ),
        compiler_params=params(16),
    )(y.reshape(1), *hbm(quarter, sent, other, eigvec, eigvec), root[None, :], root[:, None])


def first_kernel(u_ref, root_ref, g_ref, wsum_ref, first_ref):
    u = u_ref[...]
    whiten = dot3(u / root_ref[...], u, 1, 1)
    wh, wl = halves(whiten)
    wsum_ref[...] = wh.astype(F32) + wl.astype(F32)
    g = g_ref[...]
    first_ref[...] = dot(g, wh, 1, 0) + dot(g, wl, 1, 0)


def first_terms(eigvec, root, embed_grad):
    n_loc, ch = embed_grad.shape
    return pl.pallas_call(
        first_kernel,
        out_shape=(pltpu.HBM((ch, ch), F32), pltpu.HBM((n_loc, ch), F32)),
        compiler_params=params(14),
        cost_estimate=cost(6 * ch**3 + 4 * n_loc * ch * ch, 6 * n_loc * ch + 8 * ch * ch),
    )(*hbm(eigvec), root[None, :], *hbm(embed_grad))


def grad_z_kernel(u_ref, inner_ref, z_ref, first_ref, wsum_ref, mean_ref, out_ref, turned_ref, *, scale):
    u, inner = u_ref[...], inner_ref[...]
    uh, ul = halves(u)
    back = dot(uh, inner, 1, 0) + dot(ul, inner, 1, 0)
    dsigma = dot3(back, u, 1, 1) * scale
    dh, dl = halves(dsigma)
    mean = mean_ref[...]
    bias = dot3(mean, wsum_ref[...], 1, 0)[1:2] + dot3(mean, dh.astype(F32) + dl.astype(F32), 1, 0)[0:1]
    z = z_ref[...]
    out = first_ref[...] + dot(z, dh, 1, 0) + dot(z, dl, 1, 0) - bias
    out_ref[...] = bf(out)
    turned_ref[...] = bf(out.T)


def grad_z_of(eigvec, inner, embed, first, wsum, means, rows):
    n_loc, ch = embed.shape
    return pl.pallas_call(
        functools.partial(grad_z_kernel, scale=2.0 / rows),
        out_shape=(pltpu.HBM((n_loc, ch), BF16), pltpu.HBM((ch, n_loc), BF16)),
        compiler_params=params(20),
        cost_estimate=cost(10 * ch**3 + 4 * n_loc * ch * ch, 8 * n_loc * ch + 10 * ch * ch),
    )(*hbm(eigvec, inner, embed, first, wsum), means)


def ring_shapes(rows, cols):
    half = rows // 2
    return (
        pltpu.HBM((rows, cols), BF16),
        pltpu.HBM((rows, cols), BF16),
        pltpu.HBM((rows, cols), F32),
        pltpu.HBM((half, cols), F32),
        pltpu.HBM((half, cols), F32),
    )


def ring_store(r, start, acc, up_ref, down_ref, b0_ref, b1_ref, b3_ref, cols=slice(None)):
    size, half = acc.shape[0], b1_ref.shape[0]
    lower = start < half
    at = pl.ds(start % half, size)
    later = pl.ds(half + start % half, size)

    @pl.when(r == 0)
    def _():
        b0_ref[pl.ds(start, size), cols] = acc

    @pl.when(r == 1)
    def _():
        if lower:
            b1_ref[at, cols] = acc
        else:
            up_ref[at, cols] = bf(acc)

    @pl.when(r == 2)
    def _():
        if lower:
            up_ref[later, cols] = bf(acc)
        else:
            down_ref[at, cols] = bf(acc)

    @pl.when(r == 3)
    def _():
        if lower:
            down_ref[later, cols] = bf(acc)
        else:
            b3_ref[at, cols] = acc


def order_kernel(idx_ref, own_ref, right_ref, two_a_ref, two_b_ref, left_ref, out_ref, sems):
    fs = own_ref.shape[2]
    for g in range(8):
        place, side = idx_ref[g] // 2, idx_ref[g] % 2
        to, sem = out_ref.at[:, g * fs : (g + 1) * fs], sems.at[g]
        for n, ref in ((0, own_ref), (1, right_ref), (3, left_ref)):

            @pl.when(place == n)
            def _():
                pltpu.make_async_copy(ref.at[side], to, sem).start()

        for n, ref in ((0, two_a_ref), (1, two_b_ref)):

            @pl.when((place == 2) & (side == n))
            def _():
                pltpu.make_async_copy(ref.at[0], to, sem).start()

    for g in range(8):
        to, sem = out_ref.at[:, g * fs : (g + 1) * fs], sems.at[g]
        pltpu.make_async_copy(own_ref.at[0], to, sem).wait()


def in_order(sources, order):
    _, depth, fs = sources[0].shape
    return pl.pallas_call(
        order_kernel,
        out_shape=jax.ShapeDtypeStruct((depth, 8 * fs), BF16),
        in_specs=[pl.BlockSpec(memory_space=pltpu.SMEM)] + [pl.BlockSpec(memory_space=pl.ANY)] * 5,
        out_specs=pl.BlockSpec(memory_space=pl.ANY),
        scratch_shapes=[pltpu.SemaphoreType.DMA((8,))],
        compiler_params=params(4),
    )(order, *sources)


def stack_kernel(*refs):
    *sources, out_ref = refs
    at = 0
    for ref in sources:
        out_ref[at : at + ref.shape[0], :] = ref[...]
        at += ref.shape[0]


def stacked(sources):
    rows = sum(a.shape[0] for a in sources)
    return pl.pallas_call(
        stack_kernel,
        out_shape=pltpu.HBM((rows, sources[0].shape[1]), BF16),
        compiler_params=params(12),
    )(*sources)


def halves_kernel(core_ref, keep_in, give_in, keep_ref, give_ref):
    keep_ref[...] = bf(keep_in[...].astype(F32).T)
    give_ref[...] = bf(give_in[...].astype(F32).T)


def turned_halves(weight, core):
    rows, ch = weight.shape
    half = rows // 2
    shape = jax.ShapeDtypeStruct((ch, half), BF16)
    return pl.pallas_call(
        halves_kernel,
        out_shape=(shape, shape),
        grid_spec=pltpu.PrefetchScalarGridSpec(
            num_scalar_prefetch=1,
            grid=(1,),
            in_specs=[
                pl.BlockSpec((half, ch), lambda i, c: (c[0], 0)),
                pl.BlockSpec((half, ch), lambda i, c: (1 - c[0], 0)),
            ],
            out_specs=tuple(pl.BlockSpec((ch, half), lambda i, c: (0, 0)) for _ in range(2)),
        ),
        compiler_params=params(12),
    )(core.reshape(1), weight, weight)


def hidden_kernel(*refs):
    *lhs, w_ref, out_ref = refs
    _, rows, wide = out_ref.shape
    tile = rows // 2
    for start in range(0, rows, tile):
        acc, k0, seen = None, 0, 0
        for ref in lhs:
            depth = ref.shape[1]
            if seen <= start < seen + ref.shape[0]:
                term = dot(ref[start - seen : start - seen + tile, :], w_ref[k0 : k0 + depth, :], 1, 0)
                acc = term if acc is None else acc + term
            seen += ref.shape[0]
            if seen == rows:
                seen, k0 = 0, k0 + depth
        for r in range(4):
            out_ref[r, start : start + tile, :] = bf(acc[:, r * wide : (r + 1) * wide])


def hidden_terms(pieces, w_all):
    rows = pieces[0].shape[0]
    depth, wide = w_all.shape
    return pl.pallas_call(
        hidden_kernel,
        out_shape=pltpu.HBM((4, rows, wide // 4), BF16),
        compiler_params=params(20),
        cost_estimate=cost(2 * rows * wide * depth, 2 * (rows + wide) * depth + 2 * rows * wide),
    )(*pieces, w_all)


def here_kernel(idx_ref, p_ref, own_ref, out_ref):
    out_ref[...] = dot(p_ref[...], own_ref[...], 1, 0)


def weight_here(turned, hidden, order):
    ch, n_loc = turned.shape
    feat = hidden.shape[1] // 8
    return pl.pallas_call(
        here_kernel,
        out_shape=pltpu.HBM((ch, 4 * feat), F32),
        grid_spec=pltpu.PrefetchScalarGridSpec(
            num_scalar_prefetch=1,
            grid=(4,),
            in_specs=[
                pl.BlockSpec((ch, n_loc), lambda r, idx: (0, 0)),
                pl.BlockSpec((n_loc, feat), lambda r, idx: (0, idx[r])),
            ],
            out_specs=pl.BlockSpec((ch, feat), lambda r, idx: (0, r)),
        ),
        compiler_params=params(14),
        cost_estimate=cost(8 * ch * n_loc * feat, 8 * feat * (n_loc + 2 * ch)),
    )(order, *hbm(turned, hidden))


def weight_kernel(idx_ref, q_ref, own_ref, hx_ref, hk_ref, up_ref, down_ref, b0_ref, b1_ref, b3_ref, turned_ref):
    r = pl.program_id(0)
    core, x = idx_ref[4], idx_ref[5]
    half = hx_ref.shape[0]
    h = b1_ref.shape[0]
    sub = half // 4

    @pl.when(r == 0)
    def _():
        for n in range(8):
            k = core if n < 4 else 1 - core
            row = pl.multiple_of((k * 4 + (x + n) % 4) * sub, sub)
            turned_ref[:, n * sub : (n + 1) * sub] = bf(q_ref[pl.ds(row, sub), :].astype(F32).T)

    acc = own_ref[...] + dot(turned_ref[:, :half], hx_ref[...], 1, 0) + dot(turned_ref[:, half:], hk_ref[...], 1, 0)
    for start in (0, h):
        ring_store(r, start, acc[start : start + h], up_ref, down_ref, b0_ref, b1_ref, b3_ref)


def weight_terms(q_own, w_here, h_x, h_k, order):
    n_loc, ch = q_own.shape
    feat = h_x.shape[1] // 4
    shapes = ring_shapes(ch, feat)
    whole = lambda a: pl.BlockSpec(a.shape, lambda r, idx: (0, 0))
    return pl.pallas_call(
        weight_kernel,
        out_shape=shapes,
        grid_spec=pltpu.PrefetchScalarGridSpec(
            num_scalar_prefetch=1,
            grid=(4,),
            in_specs=[
                whole(q_own),
                pl.BlockSpec((ch, feat), lambda r, idx: (0, r)),
                pl.BlockSpec((n_loc // 2, feat), lambda r, idx: (0, r)),
                pl.BlockSpec((n_loc // 2, feat), lambda r, idx: (0, r)),
            ],
            out_specs=tuple(whole(a) for a in shapes),
            scratch_shapes=[pltpu.VMEM((ch, n_loc), BF16)],
        ),
        compiler_params=params(30),
        cost_estimate=cost(8 * n_loc * feat * ch, 8 * n_loc * feat + 28 * ch * feat),
    )(order, q_own, *hbm(w_here, h_x, h_k))


def ring_finish(terms, first, up, down):
    _, _, b0, b1, b3 = terms
    from_down, from_up = first
    h = b1.shape[0]
    from_down2 = up(bf(b1 + from_down[h:].astype(F32)))
    from_up2 = down(bf(b3 + from_up[:h].astype(F32)))
    lower = b0[:h] + from_up[h:].astype(F32) + from_down2.astype(F32)
    upper = b0[h:] + from_down[:h].astype(F32) + from_up2.astype(F32)
    return jnp.concatenate([lower, upper])


def local(hidden, weight, embed, embed_grad, eigvec, eigval):
    dp, chan = lax.axis_index("dp"), lax.axis_index("chan")
    zlo, y = dp // 4, dp % 4
    x, zhi, core = chan // 4, (chan // 2) % 2, chan % 2
    z = zhi * 2 + zlo
    n_loc = embed.shape[0]
    rows = n_loc * 8
    ch = embed.shape[1]
    feat = hidden.shape[1] // 8
    sub = n_loc // 8

    groups = [[0, 1, 2, 3], [4, 5, 6, 7]]
    x_groups = [[(i * 2 + a) * 2 + b for i in range(4)] for a in range(2) for b in range(2)]
    fs = weight.shape[0] // 8
    w_keep, w_give = turned_halves(weight, core)
    w_got = swap(w_give)
    wz = [
        jnp.concatenate([lax.dynamic_slice(a, (0, (z ^ j) * fs), (ch, fs)) for a in (w_keep, w_got)]) for j in range(4)
    ]
    message, hidden, *wz = tie(moments(embed, embed_grad, eigvec), hidden, *wz)
    got = lax.all_to_all(message, "dp", 0, 0, axis_index_groups=groups)

    def hidden_part(r, half, start, size):
        return lax.dynamic_slice(hidden, (start, (half * 4 + (y + r) % 4) * feat), (size, feat))

    mine = jnp.concatenate([hidden_part(r, 1 - zlo, (core * 4 + x) * sub, sub) for r in range(4)], axis=1)
    h0 = stacked([z_up(mine[: sub // 2]), z_down(mine[sub // 2 :])])
    h_left, h_right = x_up(h0), x_down(h0)
    wz = [wz[0]] + [z_flip[j](wz[j]) for j in (1, 2, 3)]
    quarter, sent = quarter_terms(got)
    other = z_flip[1](sent)
    root = jnp.sqrt(eigval)
    root, _ = tie(root, quarter)
    wsum, first = first_terms(eigvec, root, embed_grad)
    other, first, wsum, *wz = tie(other, first, wsum, *wz)
    w_own = jnp.stack([jnp.concatenate([wz[0], wz[2]]), jnp.concatenate([wz[1], wz[3]])])
    w_left, w_right = y_up(w_own), y_down(w_own)
    inner4, means = inner_terms(quarter, sent, other, eigvec, root, y, n_loc)
    inner = lax.all_to_all(inner4, "dp", 0, 0, axis_index_groups=groups).reshape(ch, ch)
    inner, h_left, h_right = tie(inner, h_left, h_right)
    h_two = x_up(h_left)
    grad_z, turned = grad_z_of(eigvec, inner, embed, first, wsum, means, rows)

    w_order = []
    for r in range(4):
        for f in range(2):
            y_s = 2 * (r % 2) + (zhi ^ f)
            w_order.append(((y_s - y) % 4) * 2 + ((r // 2) ^ zlo))
    w_order = jnp.stack(w_order).astype(jnp.int32)
    h_order = jnp.stack([zlo * 4 + (y + r) % 4 for r in range(4)] + [core, x]).astype(jnp.int32)

    ht = n_loc // 2
    r_own = z_flip[1](grad_z)
    r_oth = z_flip[3](grad_z)
    own2 = swap(grad_z)
    turned, w_left, w_right = tie(turned, w_left, w_right)
    w_here = weight_here(turned, hidden, h_order)
    w_two = y_up(w_left[:1]), y_down(w_right[1:])
    w_all = in_order([w_own, w_right, *w_two, w_left], w_order)
    h_x = stacked([h0, h_right, h_two, h_left])
    near = swap(r_own), swap(r_oth)
    r_own, r_oth, w_here, w_all, h_x, *near = tie(r_own, r_oth, w_here, w_all, h_x, *near)

    far = z_flip[1](r_oth[:ht]), z_flip[3](r_own[ht:])
    par = hidden_terms([r_own, near[0], r_oth, near[1]], w_all)
    _, h_x = tie(par, h_x)
    h_k = swap(h_x)
    par_got = lax.all_to_all(par, "chan", 0, 0, axis_index_groups=x_groups)

    r_own, _ = tie(r_own, par)
    w_terms = weight_terms(r_own, w_here, h_x, h_k, h_order)
    w_first = y_up(w_terms[0]), y_down(w_terms[1])

    grad_z, _, *far = tie(grad_z, w_terms[0], *far)
    far2 = [swap(a) for a in far]
    own = hidden_terms([grad_z, own2, *far, *far2], w_all)
    own, par_got = tie(own, par_got)
    own_got = lax.all_to_all(own, "chan", 0, 0, axis_index_groups=x_groups)
    s_par = bf(jnp.sum(par_got.astype(F32), axis=0))
    p1 = z_flip[1](s_par[:, :fs])
    p3 = z_flip[3](s_par[:, fs:])
    w_sum = ring_finish(w_terms, w_first, y_up, y_down)
    s_own = bf(jnp.sum(own_got.astype(F32), axis=0))
    p0 = s_own[:, :fs]
    p2 = z_flip[2](s_own[:, fs:])
    grad_weight = bf(w_sum.T)
    odd = zlo == 1
    u0, u1 = jnp.where(odd, p1, p0), jnp.where(odd, p0, p1)
    u2, u3 = jnp.where(odd, p3, p2), jnp.where(odd, p2, p3)
    low = jnp.concatenate([u0, u1], axis=1)
    high = jnp.concatenate([u2, u3], axis=1)
    up = zhi == 1
    grad_hidden = jnp.concatenate([jnp.where(up, high, low), jnp.where(up, low, high)], axis=1)
    return grad_weight, grad_hidden


def solution(mesh):
    in_specs = (
        P("dp", None),
        P("dp", "chan"),
        P("dp", "chan"),
        P("dp", "chan"),
        P("chan", None),
        P("chan"),
    )
    out_specs = (P("dp", "chan"), P("dp", "chan"))
    return jax.shard_map(local, mesh=mesh, in_specs=in_specs, out_specs=out_specs, check_vma=False)
```

```python
import functools

import jax
import jax.numpy as jnp
from jax import lax
from jax.experimental import pallas as pl
from jax.experimental.pallas import tpu as pltpu
from jax.sharding import PartitionSpec as P

F32 = jnp.float32
BF16 = jnp.bfloat16
AXES = ("dp", "chan")


def place_of(index):
    dp, chan = divmod(index, 16)
    zlo, y = divmod(dp, 4)
    x, rest = divmod(chan, 4)
    zhi, core = divmod(rest, 2)
    return x, y, zhi * 2 + zlo, core


def index_of(x, y, z, core):
    zhi, zlo = divmod(z % 4, 2)
    return (zlo * 4 + y % 4) * 16 + ((x % 4) * 2 + zhi) * 2 + core


def mover(step):
    pairs = [(i, index_of(*step(*place_of(i)))) for i in range(128)]
    return lambda a: lax.ppermute(a, AXES, pairs)


x_up = mover(lambda x, y, z, k: (x + 1, y, z, k))
x_down = mover(lambda x, y, z, k: (x - 1, y, z, k))
y_up = mover(lambda x, y, z, k: (x, y + 1, z, k))
y_down = mover(lambda x, y, z, k: (x, y - 1, z, k))
z_up = mover(lambda x, y, z, k: (x, y, z + 1, k))
z_down = mover(lambda x, y, z, k: (x, y, z - 1, k))
z_flip = [None] + [mover(lambda x, y, z, k, j=j: (x, y, z ^ j, k)) for j in (1, 2, 3)]
swap = mover(lambda x, y, z, k: (x, y, z, 1 - k))


def bf(a):
    return a.astype(BF16)


def tie(*arrays):
    return lax.optimization_barrier(arrays)


def halves(a):
    head = bf(a)
    return head, bf(a - head.astype(F32))


def dot(a, b, ca, cb):
    return lax.dot_general(a, b, (((ca,), (cb,)), ((), ())), preferred_element_type=F32)


def dot3(a, b, ca, cb):
    (ah, al), (bh, bl) = halves(a), halves(b)
    return dot(ah, bh, ca, cb) + (dot(ah, bl, ca, cb) + dot(al, bh, ca, cb))


def hbm(*arrays):
    return [pltpu.with_memory_space_constraint(a, pltpu.HBM) for a in arrays]


def params(mib):
    return pltpu.CompilerParams(vmem_limit_bytes=mib * 2**20)


def cost(flops, nbytes):
    return pl.CostEstimate(flops=int(flops), bytes_accessed=int(nbytes), transcendentals=0)


def moments_kernel(z_ref, g_ref, u_ref, out_ref):
    n_loc, ch = z_ref.shape
    q = ch // 4
    z, g = z_ref[...], g_ref[...]
    sum_z = jnp.sum(z.astype(F32), axis=0, keepdims=True)
    sum_g = jnp.sum(g.astype(F32), axis=0, keepdims=True)
    zero = jnp.zeros((7, ch), F32)
    outer = dot3(jnp.concatenate([sum_z * (1.0 / n_loc), zero]), jnp.concatenate([sum_g, zero]), 0, 0)
    part = dot(z, g, 0, 0) - outer
    sym = 0.5 * (part + part.T)
    u = u_ref[...]
    rotated = dot3(dot3(u, sym, 0, 0), u, 1, 0)
    sums = jnp.concatenate([sum_z, sum_g])
    parts = []
    for _ in range(3):
        head = bf(sums).astype(F32)
        parts.append(head)
        sums = sums - head
    small = bf(jnp.concatenate(parts + [jnp.zeros((10, ch), F32)]))
    for r in range(4):
        out_ref[r, :q, :] = bf(rotated[r * q : (r + 1) * q])
        out_ref[r, q:, :] = small


def moments(embed, embed_grad, eigvec):
    n_loc, ch = embed.shape
    return pl.pallas_call(
        moments_kernel,
        out_shape=pltpu.HBM((4, ch // 4 + 16, ch), BF16),
        compiler_params=params(20),
        cost_estimate=cost(2 * n_loc * ch * ch + 12 * ch**3, 4 * n_loc * ch + 6 * ch * ch),
    )(*hbm(embed, embed_grad, eigvec))


def quarter_kernel(got_ref, quarter_ref, sent_ref):
    q = quarter_ref.shape[0]
    total = sum(got_ref[r, :q, :].astype(F32) for r in range(4))
    quarter_ref[...] = total
    sent_ref[:q, :] = bf(total)
    for r in range(4):
        sent_ref[q + 16 * r : q + 16 * (r + 1), :] = got_ref[r, q:, :]


def inner_kernel(y_ref, quarter_ref, sent_ref, other_ref, u_ref, uq_ref, root_ref, rootq_ref, inner_ref, mean_ref, *, n_loc):
    q, ch = quarter_ref.shape
    first, second = [], []
    for ref in (sent_ref, other_ref):
        small = ref[q:, :].astype(F32)
        for r in range(4):
            block = small[16 * r : 16 * r + 16]
            both = block[0:2] + block[2:4] + block[4:6]
            first.append(both[0:1])
            second.append(both[1:2])
    sum_z, sum_g = jnp.concatenate(first), jnp.concatenate(second)
    mean_z = jnp.sum(sum_z, axis=0, keepdims=True) * (1.0 / (8 * n_loc))
    mean_g = jnp.sum(sum_g, axis=0, keepdims=True) * (1.0 / (8 * n_loc))
    dev_z = sum_z - n_loc * mean_z
    dev_g = sum_g * (1.0 / n_loc)
    turned = dot3(jnp.concatenate([dev_g, dev_z]), u_ref[...], 1, 0)
    turned_q = dot3(jnp.concatenate([dev_z, dev_g]), uq_ref[...], 1, 0)
    total = quarter_ref[...] + other_ref[:q, :].astype(F32) + 0.5 * dot3(turned_q, turned, 0, 0)
    root, rootq = root_ref[...], rootq_ref[...]
    inner = bf(total * (-1.0 / (rootq * root * (rootq + root))))
    for r in range(4):
        inner_ref[r] = inner
    mean_ref[...] = jnp.concatenate([mean_z, mean_g, jnp.zeros((6, ch), F32)])


def quarter_terms(got):
    ch = got.shape[2]
    q = ch // 4
    return pl.pallas_call(
        quarter_kernel,
        out_shape=(pltpu.HBM((q, ch), F32), pltpu.HBM((q + 64, ch), BF16)),
        compiler_params=params(8),
    )(*hbm(got))


def inner_terms(quarter, sent, other, eigvec, root, y, n_loc):
    q, ch = quarter.shape
    full = lambda *shape: pl.BlockSpec(shape, lambda i, y: (0,) * len(shape))
    return pl.pallas_call(
        functools.partial(inner_kernel, n_loc=n_loc),
        out_shape=(pltpu.HBM((4, q, ch), BF16), pltpu.HBM((8, ch), F32)),
        grid_spec=pltpu.PrefetchScalarGridSpec(
            num_scalar_prefetch=1,
            grid=(1,),
            in_specs=[
                full(q, ch),
                full(q + 64, ch),
                full(q + 64, ch),
                full(ch, ch),
                pl.BlockSpec((ch, q), lambda i, y: (0, y[0])),
                full(1, ch),
                pl.BlockSpec((q, 1), lambda i, y: (y[0], 0)),
            ],
            out_specs=(full(4, q, ch), full(8, ch)),
        ),
        compiler_params=params(16),
    )(y.reshape(1), *hbm(quarter, sent, other, eigvec, eigvec), root[None, :], root[:, None])


def first_kernel(u_ref, root_ref, g_ref, wsum_ref, first_ref):
    u = u_ref[...]
    whiten = dot3(u / root_ref[...], u, 1, 1)
    wh, wl = halves(whiten)
    wsum_ref[...] = wh.astype(F32) + wl.astype(F32)
    g = g_ref[...]
    first_ref[...] = dot(g, wh, 1, 0) + dot(g, wl, 1, 0)


def first_terms(eigvec, root, embed_grad):
    n_loc, ch = embed_grad.shape
    return pl.pallas_call(
        first_kernel,
        out_shape=(pltpu.HBM((ch, ch), F32), pltpu.HBM((n_loc, ch), F32)),
        compiler_params=params(14),
        cost_estimate=cost(6 * ch**3 + 4 * n_loc * ch * ch, 6 * n_loc * ch + 8 * ch * ch),
    )(*hbm(eigvec), root[None, :], *hbm(embed_grad))


def grad_z_kernel(u_ref, inner_ref, z_ref, first_ref, wsum_ref, mean_ref, out_ref, turned_ref, *, scale):
    u, inner = u_ref[...], inner_ref[...]
    uh, ul = halves(u)
    back = dot(uh, inner, 1, 0) + dot(ul, inner, 1, 0)
    dsigma = dot3(back, u, 1, 1) * scale
    dh, dl = halves(dsigma)
    mean = mean_ref[...]
    bias = dot3(mean, wsum_ref[...], 1, 0)[1:2] + dot3(mean, dh.astype(F32) + dl.astype(F32), 1, 0)[0:1]
    z = z_ref[...]
    out = first_ref[...] + dot(z, dh, 1, 0) + dot(z, dl, 1, 0) - bias
    out_ref[...] = bf(out)
    turned_ref[...] = bf(out.T)


def grad_z_of(eigvec, inner, embed, first, wsum, means, rows):
    n_loc, ch = embed.shape
    return pl.pallas_call(
        functools.partial(grad_z_kernel, scale=2.0 / rows),
        out_shape=(pltpu.HBM((n_loc, ch), BF16), pltpu.HBM((ch, n_loc), BF16)),
        compiler_params=params(20),
        cost_estimate=cost(10 * ch**3 + 4 * n_loc * ch * ch, 8 * n_loc * ch + 10 * ch * ch),
    )(*hbm(eigvec, inner, embed, first, wsum), means)


def ring_shapes(rows, cols):
    half = rows // 2
    return (
        pltpu.HBM((rows, cols), BF16),
        pltpu.HBM((rows, cols), BF16),
        pltpu.HBM((rows, cols), F32),
        pltpu.HBM((half, cols), F32),
        pltpu.HBM((half, cols), F32),
    )


def ring_store(r, start, acc, up_ref, down_ref, b0_ref, b1_ref, b3_ref, cols=slice(None)):
    size, half = acc.shape[0], b1_ref.shape[0]
    lower = start < half
    at = pl.ds(start % half, size)
    later = pl.ds(half + start % half, size)

    @pl.when(r == 0)
    def _():
        b0_ref[pl.ds(start, size), cols] = acc

    @pl.when(r == 1)
    def _():
        if lower:
            b1_ref[at, cols] = acc
        else:
            up_ref[at, cols] = bf(acc)

    @pl.when(r == 2)
    def _():
        if lower:
            up_ref[later, cols] = bf(acc)
        else:
            down_ref[at, cols] = bf(acc)

    @pl.when(r == 3)
    def _():
        if lower:
            down_ref[later, cols] = bf(acc)
        else:
            b3_ref[at, cols] = acc


def order_kernel(idx_ref, own_ref, right_ref, two_a_ref, two_b_ref, left_ref, out_ref, sems):
    fs = own_ref.shape[2]
    for g in range(8):
        place, side = idx_ref[g] // 2, idx_ref[g] % 2
        to, sem = out_ref.at[:, g * fs : (g + 1) * fs], sems.at[g]
        for n, ref in ((0, own_ref), (1, right_ref), (3, left_ref)):

            @pl.when(place == n)
            def _():
                pltpu.make_async_copy(ref.at[side], to, sem).start()

        for n, ref in ((0, two_a_ref), (1, two_b_ref)):

            @pl.when((place == 2) & (side == n))
            def _():
                pltpu.make_async_copy(ref.at[0], to, sem).start()

    for g in range(8):
        to, sem = out_ref.at[:, g * fs : (g + 1) * fs], sems.at[g]
        pltpu.make_async_copy(own_ref.at[0], to, sem).wait()


def in_order(sources, order):
    _, depth, fs = sources[0].shape
    return pl.pallas_call(
        order_kernel,
        out_shape=jax.ShapeDtypeStruct((depth, 8 * fs), BF16),
        in_specs=[pl.BlockSpec(memory_space=pltpu.SMEM)] + [pl.BlockSpec(memory_space=pl.ANY)] * 5,
        out_specs=pl.BlockSpec(memory_space=pl.ANY),
        scratch_shapes=[pltpu.SemaphoreType.DMA((8,))],
        compiler_params=params(4),
    )(order, *sources)


def stack_kernel(*refs):
    *sources, out_ref = refs
    at = 0
    for ref in sources:
        out_ref[at : at + ref.shape[0], :] = ref[...]
        at += ref.shape[0]


def stacked(sources):
    rows, wide = sum(a.shape[0] for a in sources), sources[0].shape[1]
    block = lambda n: pl.BlockSpec((n, wide // 4), lambda c: (0, c))
    return pl.pallas_call(
        stack_kernel,
        out_shape=pltpu.HBM((rows, wide), BF16),
        grid=(4,),
        in_specs=[block(a.shape[0]) for a in sources],
        out_specs=block(rows),
        compiler_params=params(12),
    )(*sources)


def halves_kernel(core_ref, keep_in, give_in, keep_ref, give_ref):
    keep_ref[...] = bf(keep_in[...].astype(F32).T)
    give_ref[...] = bf(give_in[...].astype(F32).T)


def turned_halves(weight, core):
    rows, ch = weight.shape
    half = rows // 2
    shape = jax.ShapeDtypeStruct((ch, half), BF16)
    return pl.pallas_call(
        halves_kernel,
        out_shape=(shape, shape),
        grid_spec=pltpu.PrefetchScalarGridSpec(
            num_scalar_prefetch=1,
            grid=(1,),
            in_specs=[
                pl.BlockSpec((half, ch), lambda i, c: (c[0], 0)),
                pl.BlockSpec((half, ch), lambda i, c: (1 - c[0], 0)),
            ],
            out_specs=tuple(pl.BlockSpec((ch, half), lambda i, c: (0, 0)) for _ in range(2)),
        ),
        compiler_params=params(12),
    )(core.reshape(1), weight, weight)


def hidden_kernel(*refs):
    *lhs, w_ref, out_ref = refs
    _, rows, wide = out_ref.shape
    tile = rows // 2
    for start in range(0, rows, tile):
        acc, k0, seen = None, 0, 0
        for ref in lhs:
            depth = ref.shape[1]
            if seen <= start < seen + ref.shape[0]:
                term = dot(ref[start - seen : start - seen + tile, :], w_ref[k0 : k0 + depth, :], 1, 0)
                acc = term if acc is None else acc + term
            seen += ref.shape[0]
            if seen == rows:
                seen, k0 = 0, k0 + depth
        for r in range(4):
            out_ref[r, start : start + tile, :] = bf(acc[:, r * wide : (r + 1) * wide])


def hidden_terms(pieces, w_all):
    rows = pieces[0].shape[0]
    depth, wide = w_all.shape
    return pl.pallas_call(
        hidden_kernel,
        out_shape=pltpu.HBM((4, rows, wide // 4), BF16),
        compiler_params=params(20),
        cost_estimate=cost(2 * rows * wide * depth, 2 * (rows + wide) * depth + 2 * rows * wide),
    )(*pieces, w_all)


def here_kernel(idx_ref, p_ref, own_ref, out_ref):
    out_ref[...] = dot(p_ref[...], own_ref[...], 1, 0)


def weight_here(turned, hidden, order):
    ch, n_loc = turned.shape
    feat = hidden.shape[1] // 8
    return pl.pallas_call(
        here_kernel,
        out_shape=pltpu.HBM((ch, 4 * feat), F32),
        grid_spec=pltpu.PrefetchScalarGridSpec(
            num_scalar_prefetch=1,
            grid=(4,),
            in_specs=[
                pl.BlockSpec((ch, n_loc), lambda r, idx: (0, 0)),
                pl.BlockSpec((n_loc, feat), lambda r, idx: (0, idx[r])),
            ],
            out_specs=pl.BlockSpec((ch, feat), lambda r, idx: (0, r)),
        ),
        compiler_params=params(14),
        cost_estimate=cost(8 * ch * n_loc * feat, 8 * feat * (n_loc + 2 * ch)),
    )(order, *hbm(turned, hidden))


def weight_kernel(idx_ref, q_ref, own_ref, hx_ref, hk_ref, up_ref, down_ref, b0_ref, b1_ref, b3_ref, turned_ref):
    r = pl.program_id(0)
    core, x = idx_ref[4], idx_ref[5]
    half = hx_ref.shape[0]
    h = b1_ref.shape[0]
    sub = half // 4

    @pl.when(r == 0)
    def _():
        for n in range(8):
            k = core if n < 4 else 1 - core
            row = pl.multiple_of((k * 4 + (x + n) % 4) * sub, sub)
            turned_ref[:, n * sub : (n + 1) * sub] = bf(q_ref[pl.ds(row, sub), :].astype(F32).T)

    acc = own_ref[...] + dot(turned_ref[:, :half], hx_ref[...], 1, 0) + dot(turned_ref[:, half:], hk_ref[...], 1, 0)
    for start in (0, h):
        ring_store(r, start, acc[start : start + h], up_ref, down_ref, b0_ref, b1_ref, b3_ref)


def weight_terms(q_own, w_here, h_x, h_k, order):
    n_loc, ch = q_own.shape
    feat = h_x.shape[1] // 4
    shapes = ring_shapes(ch, feat)
    whole = lambda a: pl.BlockSpec(a.shape, lambda r, idx: (0, 0))
    return pl.pallas_call(
        weight_kernel,
        out_shape=shapes,
        grid_spec=pltpu.PrefetchScalarGridSpec(
            num_scalar_prefetch=1,
            grid=(4,),
            in_specs=[
                whole(q_own),
                pl.BlockSpec((ch, feat), lambda r, idx: (0, r)),
                pl.BlockSpec((n_loc // 2, feat), lambda r, idx: (0, r)),
                pl.BlockSpec((n_loc // 2, feat), lambda r, idx: (0, r)),
            ],
            out_specs=tuple(whole(a) for a in shapes),
            scratch_shapes=[pltpu.VMEM((ch, n_loc), BF16)],
        ),
        compiler_params=params(30),
        cost_estimate=cost(8 * n_loc * feat * ch, 8 * n_loc * feat + 28 * ch * feat),
    )(order, q_own, *hbm(w_here, h_x, h_k))


def ring_finish(terms, first, up, down):
    _, _, b0, b1, b3 = terms
    from_down, from_up = first
    h = b1.shape[0]
    from_down2 = up(bf(b1 + from_down[h:].astype(F32)))
    from_up2 = down(bf(b3 + from_up[:h].astype(F32)))
    lower = b0[:h] + from_up[h:].astype(F32) + from_down2.astype(F32)
    upper = b0[h:] + from_down[:h].astype(F32) + from_up2.astype(F32)
    return jnp.concatenate([lower, upper])


def local(hidden, weight, embed, embed_grad, eigvec, eigval):
    dp, chan = lax.axis_index("dp"), lax.axis_index("chan")
    zlo, y = dp // 4, dp % 4
    x, zhi, core = chan // 4, (chan // 2) % 2, chan % 2
    z = zhi * 2 + zlo
    n_loc = embed.shape[0]
    rows = n_loc * 8
    ch = embed.shape[1]
    feat = hidden.shape[1] // 8
    sub = n_loc // 8

    groups = [[0, 1, 2, 3], [4, 5, 6, 7]]
    x_groups = [[(i * 2 + a) * 2 + b for i in range(4)] for a in range(2) for b in range(2)]
    fs = weight.shape[0] // 8
    w_keep, w_give = turned_halves(weight, core)
    w_got = swap(w_give)
    wz = [
        jnp.concatenate([lax.dynamic_slice(a, (0, (z ^ j) * fs), (ch, fs)) for a in (w_keep, w_got)]) for j in range(4)
    ]
    message, hidden, *wz = tie(moments(embed, embed_grad, eigvec), hidden, *wz)
    got = lax.all_to_all(message, "dp", 0, 0, axis_index_groups=groups)

    def hidden_part(r, half, start, size):
        return lax.dynamic_slice(hidden, (start, (half * 4 + (y + r) % 4) * feat), (size, feat))

    mine = jnp.concatenate([hidden_part(r, 1 - zlo, (core * 4 + x) * sub, sub) for r in range(4)], axis=1)
    h0 = stacked([z_up(mine[: sub // 2]), z_down(mine[sub // 2 :])])
    h_left, h_right = x_up(h0), x_down(h0)
    wz = [wz[0]] + [z_flip[j](wz[j]) for j in (1, 2, 3)]
    quarter, sent = quarter_terms(got)
    other = z_flip[1](sent)
    root = jnp.sqrt(eigval)
    root, _ = tie(root, quarter)
    wsum, first = first_terms(eigvec, root, embed_grad)
    other, first, wsum, *wz = tie(other, first, wsum, *wz)
    w_own = jnp.stack([jnp.concatenate([wz[0], wz[2]]), jnp.concatenate([wz[1], wz[3]])])
    w_left, w_right = y_up(w_own), y_down(w_own)
    inner4, means = inner_terms(quarter, sent, other, eigvec, root, y, n_loc)
    inner = lax.all_to_all(inner4, "dp", 0, 0, axis_index_groups=groups).reshape(ch, ch)
    inner, h_left, h_right = tie(inner, h_left, h_right)
    h_two = x_up(h_left)
    grad_z, turned = grad_z_of(eigvec, inner, embed, first, wsum, means, rows)

    w_order = []
    for r in range(4):
        for f in range(2):
            y_s = 2 * (r % 2) + (zhi ^ f)
            w_order.append(((y_s - y) % 4) * 2 + ((r // 2) ^ zlo))
    w_order = jnp.stack(w_order).astype(jnp.int32)
    h_order = jnp.stack([zlo * 4 + (y + r) % 4 for r in range(4)] + [core, x]).astype(jnp.int32)

    ht = n_loc // 2
    r_own = z_flip[1](grad_z)
    r_oth = z_flip[3](grad_z)
    own2 = swap(grad_z)
    turned, w_left, w_right = tie(turned, w_left, w_right)
    w_here = weight_here(turned, hidden, h_order)
    w_two = y_up(w_left[:1]), y_down(w_right[1:])
    w_all = in_order([w_own, w_right, *w_two, w_left], w_order)
    h_x = stacked([h0, h_right, h_two, h_left])
    r_own, r_oth, w_here, w_all, h_x = tie(r_own, r_oth, w_here, w_all, h_x)

    far = z_flip[1](r_oth[:ht]), z_flip[3](r_own[ht:])
    par = hidden_terms([r_own, swap(r_own), r_oth, swap(r_oth)], w_all)
    _, h_x = tie(par, h_x)
    h_k = swap(h_x)
    par_got = lax.all_to_all(par, "chan", 0, 0, axis_index_groups=x_groups)

    r_own, _ = tie(r_own, par)
    w_terms = weight_terms(r_own, w_here, h_x, h_k, h_order)
    w_first = y_up(w_terms[0]), y_down(w_terms[1])

    grad_z, _, *far = tie(grad_z, w_terms[0], *far)
    far2 = [swap(a) for a in far]
    own = hidden_terms([grad_z, own2, *far, *far2], w_all)
    own, par_got = tie(own, par_got)
    own_got = lax.all_to_all(own, "chan", 0, 0, axis_index_groups=x_groups)
    s_par = bf(jnp.sum(par_got.astype(F32), axis=0))
    p1 = z_flip[1](s_par[:, :fs])
    p3 = z_flip[3](s_par[:, fs:])
    w_sum = ring_finish(w_terms, w_first, y_up, y_down)
    s_own = bf(jnp.sum(own_got.astype(F32), axis=0))
    p0 = s_own[:, :fs]
    p2 = z_flip[2](s_own[:, fs:])
    grad_weight = bf(w_sum.T)
    odd = zlo == 1
    u0, u1 = jnp.where(odd, p1, p0), jnp.where(odd, p0, p1)
    u2, u3 = jnp.where(odd, p3, p2), jnp.where(odd, p2, p3)
    low = jnp.concatenate([u0, u1], axis=1)
    high = jnp.concatenate([u2, u3], axis=1)
    up = zhi == 1
    grad_hidden = jnp.concatenate([jnp.where(up, high, low), jnp.where(up, low, high)], axis=1)
    return grad_weight, grad_hidden


def solution(mesh):
    in_specs = (
        P("dp", None),
        P("dp", "chan"),
        P("dp", "chan"),
        P("dp", "chan"),
        P("chan", None),
        P("chan"),
    )
    out_specs = (P("dp", "chan"), P("dp", "chan"))
    return jax.shard_map(local, mesh=mesh, in_specs=in_specs, out_specs=out_specs, check_vma=False)
```
